256 devices in a mesh: ctx: 16 (over z_hi, y), head: 16 (over z_lo, x, core).
Axes of the slice: x: 4, y: 4, z: 8 (z_hi: 4, z_lo: 2; z = z_hi * 2 + z_lo), core: 2. Of those that a mesh axis runs over, the one named last changes fastest.
Arguments:
- inputs: bfloat16 [4096, 5376], P('ctx', 'head'), may hold values from -48 to 48
- positions: int32 [4096], P('ctx'), may hold values from 0 to 4095, as said below
- w_query: bfloat16 [5376, 4096], P(None, 'head'), may hold values from -0.125 to 0.125
- w_key: bfloat16 [5376, 2048], P(None, 'head'), may hold values from -0.125 to 0.125
- w_value: bfloat16 [5376, 2048], P(None, 'head'), may hold values from -0.078125 to 0.078125
- w_out: bfloat16 [4096, 5376], P('head'), may hold values from -1 to 1
- post_gain: bfloat16 [5376], P('head'), may hold values from 0.25 to 1.75
- cotangent: bfloat16 [4096, 5376], P('ctx', 'head'), may hold values from -6 to 6
Outputs:
- hidden: bfloat16 [4096, 5376], P('ctx', 'head')
- grad_inputs: bfloat16 [4096, 5376], P('ctx', 'head')
- grad_w_query: float32 [5376, 4096], P('ctx', 'head')
- grad_w_key: float32 [5376, 2048], P('ctx', 'head')
- grad_w_value: float32 [5376, 2048], P('ctx', 'head')
- grad_w_out: float32 [4096, 5376], P('head', 'ctx')
The draws below stay inside these ranges and needn't reach their ends.
Inputs may be any that keep to these rules, and one draw needn't show every extreme that they name: positions rise by one from each token to the next, except at the first token of a new document, where they are 0; the first token may lie in a document that began earlier.
All inputs are finite; a program needn't handle non-finite values.
Results may differ from the reference program's by a relative error of at most 0.02.
Values may be sent and summed in bfloat16 or wider, within the bound.
A program may use at most 128 MiB of HBM per device.

```python
import math
import jax
import jax.numpy as jnp
from jax import lax

D = 5376
HEADS = 32
KV_HEADS = 16
HEAD_DIM = 128
WINDOW = 1024
TOK_DEV = 256
TOKENS = 4096
N_CTX = 16
N_HEAD = 16


def draw_inputs(key, part):
    base_key = jax.random.fold_in(key, 101)
    noise_part = jax.random.normal(jax.random.fold_in(base_key, 1), (TOKENS, D), jnp.float32)
    return jnp.clip(noise_part, -6.0, 6.0).astype(jnp.bfloat16)


def draw_positions(key, part):
    base_key = jax.random.fold_in(key, 505)
    offset = jax.random.randint(jax.random.fold_in(base_key, 1), (), 0, TOKENS)
    first_restart = TOKENS - offset
    room = jnp.maximum(TOKENS - first_restart, 1)
    later = first_restart + jax.random.randint(jax.random.fold_in(base_key, 2), (3,), 0, 1 << 30) % room
    restarts = jnp.concatenate([first_restart[None], later]).astype(jnp.int32)
    row_index = jnp.arange(TOKENS, dtype=jnp.int32)
    last_start = jnp.max(jnp.where(restarts[None, :] <= row_index[:, None], restarts[None, :], -offset), axis=1)
    return (row_index - last_start).astype(jnp.int32)


def query_base(key):
    base_key = jax.random.fold_in(key, 202)
    values = jax.random.normal(base_key, (D, HEADS * HEAD_DIM), jnp.float32)
    return values * D ** (-0.5)


def draw_w_query(key, part):
    return jnp.clip(query_base(key), -0.125, 0.125).astype(jnp.bfloat16)


def draw_w_key(key, part):
    own_part = jax.random.normal(jax.random.fold_in(key, 303), (D, KV_HEADS * HEAD_DIM), jnp.float32) * D ** (-0.5)
    return jnp.clip(own_part, -0.125, 0.125).astype(jnp.bfloat16)


def draw_w_out(key, part):
    base_key = jax.random.fold_in(key, 404)
    columns = jnp.arange(D, dtype=jnp.float32)[None, :] / (D - 1)
    values = jax.random.normal(base_key, (HEADS * HEAD_DIM, D), jnp.float32) * jnp.exp(math.log(10.0) * columns)
    return jnp.clip(values * (HEADS * HEAD_DIM) ** (-0.5), -1.0, 1.0).astype(jnp.bfloat16)


def level_of(own_key, shape, shards, least, largest):
    def one(axis_at, parts):
        steps = jax.random.uniform(jax.random.fold_in(jax.random.fold_in(own_key, 6), axis_at), (parts,), jnp.float32, least / len(shards), largest / len(shards))
        return jnp.repeat(jnp.exp(steps), shape[axis_at] // parts).reshape((-1,) + (1,) * (len(shape) - axis_at - 1))

    gain = one(*shards[0])
    for cut in shards[1:]:
        gain = gain * one(*cut)
    return gain


def bell_draw(rng, shape, deviation, most, cuts=(), kind=jnp.bfloat16):
    entries = jax.random.normal(rng, shape, jnp.float32) * deviation
    if len(cuts) > 0:
        entries = level_of(rng, shape, cuts, -0.22, 0.18) * entries
    return jnp.clip(entries, min=-most, max=most).astype(kind)


def setup_inputs(seed: int = 0) -> dict:
    streams_of = jax.random.split(jax.random.key(seed), 9)
    inputs = draw_inputs(jax.random.fold_in(streams_of[8], 71), 0)
    positions = draw_positions(jax.random.fold_in(streams_of[8], 71), 0)
    w_query = draw_w_query(jax.random.fold_in(streams_of[8], 71), 0)
    w_key = draw_w_key(jax.random.fold_in(streams_of[8], 71), 0)
    w_value = bell_draw(streams_of[4], (D, KV_HEADS * HEAD_DIM), D ** -0.5, 0.078125, ((1, 16),))
    w_out = draw_w_out(jax.random.fold_in(streams_of[8], 71), 0)
    post_gain = jnp.clip(1.0 + 0.15 * jax.random.normal(streams_of[6], (D,), jnp.float32), 0.25, 1.75).astype(jnp.bfloat16)
    cotangent = bell_draw(streams_of[7], (TOKENS, D), 1.0, 6.0, ((0, 16), (1, 16)))
    return {"inputs": inputs, "positions": positions, "w_query": w_query, "w_key": w_key, "w_value": w_value, "w_out": w_out, "post_gain": post_gain, "cotangent": cotangent}


EPSILON = 1e-06
ROPE_BASE = 10000.0

def rope_tables(positions, head_dim):
    half_dim = head_dim // 2
    frequency = jnp.exp(jnp.arange(half_dim, dtype=jnp.float32) * (-2.0 * math.log(ROPE_BASE) / head_dim))
    angles = positions.astype(jnp.float32)[:, None] * frequency[None, :]
    return (jnp.cos(angles)[:, None, :], jnp.sin(angles)[:, None, :])

def rotate(values, cosine, sine_table):
    half_dim = values.shape[-1] // 2
    first_half = values[..., :half_dim]
    second_half = values[..., half_dim:]
    return jnp.concatenate([first_half * cosine - second_half * sine_table, second_half * cosine + first_half * sine_table], axis=-1)

def window_mask(query_first, key_first, query_count, key_count, positions, window):
    query_index = query_first + jnp.arange(query_count, dtype=jnp.int32)
    key_index = key_first + jnp.arange(key_count, dtype=jnp.int32)
    distance = query_index[:, None] - key_index[None, :]
    return (key_index[None, :] >= 0) & (distance >= 0) & (distance < window) & (distance <= positions[:, None])

def widen(values):
    return lax.optimization_barrier(values).astype(jnp.float32)

def attend_forward(queries, key_block, value_block, allowed, score_scale):
    scores = jnp.einsum('tkgh,skh->kgts', widen(queries), widen(key_block)) * score_scale
    scores = jnp.where(allowed, scores, -jnp.inf)
    highest = lax.optimization_barrier(jnp.max(scores, axis=-1, keepdims=True))
    exponent = jnp.exp(scores - highest)
    probability = exponent / lax.optimization_barrier(jnp.sum(exponent, axis=-1, keepdims=True))
    weights = probability.astype(jnp.bfloat16)
    attended = jnp.einsum('kgts,skh->tkgh', widen(weights), widen(value_block)).astype(jnp.bfloat16)
    return (probability, weights, attended)

def attend_backward(queries, key_block, value_block, probability, weights, grad_attended, score_scale):
    grad_weights = jnp.einsum('tkgh,skh->kgts', widen(grad_attended), widen(value_block))
    inner = lax.optimization_barrier(jnp.sum(probability * grad_weights, axis=-1, keepdims=True))
    grad_scores = (probability * (grad_weights - inner)).astype(jnp.bfloat16)
    grad_query_part = jnp.einsum('kgts,skh->tkgh', widen(grad_scores), widen(key_block)) * score_scale
    grad_key_part = jnp.einsum('kgts,tkgh->skh', widen(grad_scores), widen(queries)) * score_scale
    grad_value_part = jnp.einsum('kgts,tkgh->skh', widen(weights), widen(grad_attended))
    return (grad_query_part, grad_key_part, grad_value_part)

def reference(inputs, positions, w_query, w_key, w_value, w_out, post_gain, cotangent):
    total_rows = inputs.shape[0]
    group_size = HEADS // KV_HEADS
    score_scale = (D // HEADS) ** (-0.5)
    span_rows = WINDOW + TOK_DEV
    cosine, sine_table = rope_tables(positions, HEAD_DIM)
    queries = rotate(jnp.dot(inputs, w_query, preferred_element_type=jnp.float32).reshape(total_rows, HEADS, HEAD_DIM), cosine, sine_table).astype(jnp.bfloat16)
    keys_all = rotate(jnp.dot(inputs, w_key, preferred_element_type=jnp.float32).reshape(total_rows, KV_HEADS, HEAD_DIM), cosine, sine_table).astype(jnp.bfloat16)
    values_all = jnp.dot(inputs, w_value, preferred_element_type=jnp.float32).astype(jnp.bfloat16).reshape(total_rows, KV_HEADS, HEAD_DIM)
    grouped = queries.reshape(total_rows, KV_HEADS, group_size, HEAD_DIM)
    padding = jnp.zeros((WINDOW, KV_HEADS, HEAD_DIM), jnp.bfloat16)
    padded_keys = jnp.concatenate([padding, keys_all], axis=0)
    padded_values = jnp.concatenate([padding, values_all], axis=0)
    blocks = jnp.arange(N_CTX, dtype=jnp.int32)

    def block_inputs(block):
        query_first = block * TOK_DEV
        block_queries = lax.dynamic_slice_in_dim(grouped, query_first, TOK_DEV, 0)
        key_block = lax.dynamic_slice_in_dim(padded_keys, query_first, span_rows, 0)
        value_block = lax.dynamic_slice_in_dim(padded_values, query_first, span_rows, 0)
        block_positions = lax.dynamic_slice_in_dim(positions, query_first, TOK_DEV, 0)
        allowed = window_mask(query_first, query_first - WINDOW, TOK_DEV, span_rows, block_positions, WINDOW)
        return (block_queries, key_block, value_block, allowed)

    def forward_block(block):
        block_queries, key_block, value_block, allowed = block_inputs(block)
        probability, weights, attended = attend_forward(block_queries, key_block, value_block, allowed, score_scale)
        return attended
    attended = lax.map(forward_block, blocks).reshape(total_rows, HEADS * HEAD_DIM)
    query_cols = HEADS * HEAD_DIM // N_HEAD
    key_cols = KV_HEADS * HEAD_DIM // N_HEAD
    branch = jnp.zeros((total_rows, D), jnp.float32)
    for head_group in range(N_HEAD):
        lower = head_group * query_cols
        partial_value = jnp.dot(attended[:, lower:lower + query_cols], w_out[lower:lower + query_cols], preferred_element_type=jnp.float32).astype(jnp.bfloat16)
        branch = branch + widen(partial_value)
    inverse_norm = lax.rsqrt(lax.optimization_barrier(jnp.sum(branch * branch, axis=1)) / D + EPSILON)
    normed = branch * inverse_norm[:, None]
    gain_all = post_gain.astype(jnp.float32)
    hidden = (inputs.astype(jnp.float32) + normed * gain_all[None, :]).astype(jnp.bfloat16)
    scaled_grad = cotangent.astype(jnp.float32) * gain_all[None, :]
    slopes = lax.optimization_barrier(jnp.sum(scaled_grad * normed, axis=1))
    branch_grad = (inverse_norm[:, None] * (scaled_grad - normed * (slopes / D)[:, None])).astype(jnp.bfloat16)
    grad_attended = jnp.dot(branch_grad, w_out.T, preferred_element_type=jnp.float32).astype(jnp.bfloat16)
    grad_w_out = jnp.dot(attended.T, branch_grad, preferred_element_type=jnp.float32)
    grad_grouped = grad_attended.reshape(total_rows, KV_HEADS, group_size, HEAD_DIM)

    def backward_block(sums, block):
        block_queries, key_block, value_block, allowed = block_inputs(block)
        probability, weights, attended_unused = attend_forward(block_queries, key_block, value_block, allowed, score_scale)
        block_grads = lax.dynamic_slice_in_dim(grad_grouped, block * TOK_DEV, TOK_DEV, 0)
        grad_query_part, grad_key_part, grad_value_part = attend_backward(block_queries, key_block, value_block, probability, weights, block_grads, score_scale)
        current = lax.dynamic_slice_in_dim(sums, block * TOK_DEV, span_rows, 1)
        sums = lax.dynamic_update_slice_in_dim(sums, current + jnp.stack([grad_key_part, grad_value_part]), block * TOK_DEV, 1)
        return (sums, grad_query_part)
    start_sums = jnp.zeros((2, WINDOW + total_rows, KV_HEADS, HEAD_DIM), jnp.float32)
    sums, query_grad_blocks = lax.scan(backward_block, start_sums, blocks)
    grad_key_rows = rotate(sums[0, WINDOW:], cosine, -sine_table).astype(jnp.bfloat16).reshape(total_rows, KV_HEADS * HEAD_DIM)
    grad_value_rows = sums[1, WINDOW:].astype(jnp.bfloat16).reshape(total_rows, KV_HEADS * HEAD_DIM)
    grad_query_rows = rotate(query_grad_blocks.reshape(total_rows, HEADS, HEAD_DIM), cosine, -sine_table).astype(jnp.bfloat16).reshape(total_rows, HEADS * HEAD_DIM)
    input_sum = jnp.zeros((total_rows, D), jnp.float32)
    for head_group in range(N_HEAD):
        query_low = head_group * query_cols
        key_low = head_group * key_cols
        term = jnp.dot(grad_query_rows[:, query_low:query_low + query_cols], w_query[:, query_low:query_low + query_cols].T, preferred_element_type=jnp.float32)
        term = term + jnp.dot(grad_key_rows[:, key_low:key_low + key_cols], w_key[:, key_low:key_low + key_cols].T, preferred_element_type=jnp.float32)
        term = term + jnp.dot(grad_value_rows[:, key_low:key_low + key_cols], w_value[:, key_low:key_low + key_cols].T, preferred_element_type=jnp.float32)
        input_sum = input_sum + widen(term.astype(jnp.bfloat16))
    grad_inputs = (cotangent.astype(jnp.float32) + input_sum).astype(jnp.bfloat16)
    grad_w_query = jnp.dot(inputs.T, grad_query_rows, preferred_element_type=jnp.float32)
    grad_w_key = jnp.dot(inputs.T, grad_key_rows, preferred_element_type=jnp.float32)
    grad_w_value = jnp.dot(inputs.T, grad_value_rows, preferred_element_type=jnp.float32)
    return (hidden, grad_inputs, grad_w_query, grad_w_key, grad_w_value, grad_w_out)
```

```python
import functools
import math

import jax
import jax.numpy as jnp
from jax import lax
from jax.experimental import pallas as pl
from jax.experimental.pallas import tpu as pltpu
from jax.sharding import PartitionSpec as P

D = 5376
HEADS = 32
WINDOW = 1024
EPSILON = 1e-06
ROPE_BASE = 10000.0
HD = 128
T = 256
BLK = 336
PAIR = 672
MESH = pl.DeviceIdType.MESH
F32 = jnp.float32
BF16 = jnp.bfloat16
SCALE = (D // HEADS) ** (-0.5)
STEP = 32


def dot_nn(a, b):
    return lax.dot_general(a, b, (((1,), (0,)), ((), ())), preferred_element_type=F32)


def dot_nt(a, b):
    return lax.dot_general(a, b, (((1,), (1,)), ((), ())), preferred_element_type=F32)


def dot_tn(a, b):
    return lax.dot_general(a, b, (((0,), (0,)), ((), ())), preferred_element_type=F32)


def rot(v, cos, sin):
    half = HD // 2
    a, b = v[:half], v[half:]
    return jnp.concatenate([a * cos - b * sin, b * cos + a * sin], axis=0)


def fold(v):
    total = v[0:8]
    for i in range(8, v.shape[0], 8):
        total = total + v[i : i + 8]
    return total


def kernel(
    x_ref, cot_ref, pos_ref, cos_ref, sin_ref, gain_ref, wq_hbm, wk_hbm, wv_hbm, wo_hbm,
    hidden_ref, gin_ref, dwq_ref, dwk_ref, dwv_ref, dwo_ref,
    w, wo, wot, xt, xa, part, bg, bgt, att_all, att, qt, ga, kv, s_scr, p_scr, wt_scr, g_all,
    acc, r_core, r_x, r_x2, r_z, s_buf, branch, stat, halo_out, halo_in, halo_prev, halo_z, dw_out, dw_in,
    load_sem, ag_s, ag_r, rs_s, rs_r, st_s, st_r, kv_s, kv_r, xa_s, xa_r, at_s, at_r, pm_s, pm_r,
    ha_s, ha_r, g_s, g_r, dw_s, dw_r,
):
    c = lax.axis_index("ctx")
    h = lax.axis_index("head")
    zh, y = c // 4, c % 4
    zl, x, q = h // 8, (h // 2) % 4, h % 2

    def head_of(o):
        return ((zl + o[0]) % 2) * 8 + ((x + o[1]) % 4) * 2 + (q + o[2]) % 2

    def at_head(o):
        return (c, head_of(o))

    def at_y(r):
        return (zh * 4 + (y + r) % 4, h)

    def at_z(r):
        return (((zh + r) % 4) * 4 + y, h)

    def rows(index, size=BLK):
        return pl.ds(pl.multiple_of(index * size, 16), size)

    pending = []

    def push(src, dst, ssem, rsem, device):
        copy = pltpu.make_async_remote_copy(
            src_ref=src, dst_ref=dst, send_sem=ssem, recv_sem=rsem, device_id=device, device_id_type=MESH
        )
        copy.start()
        return copy

    def send(*args):
        pending.append(push(*args))

    def landed(dst, ssem, rsem):
        pltpu.make_async_remote_copy(
            src_ref=dst, dst_ref=dst, send_sem=ssem, recv_sem=rsem, device_id=at_y(1), device_id_type=MESH
        ).wait_recv()

    loads = []
    for i, (src, dst) in enumerate(
        (
            (wq_hbm, w.at[:, 0:256]),
            (wk_hbm, w.at[:, 256:384]),
            (wv_hbm, w.at[:, 384:512]),
            (wo_hbm, wo),
        )
    ):
        cp = pltpu.make_async_copy(src, dst, load_sem.at[i])
        cp.start()
        loads.append(cp)
    xt[rows(h), :] = x_ref[...]

    barrier = pltpu.get_barrier_semaphore()
    others = [(a, b, d) for a in (0, 1) for b in range(4) for d in (0, 1) if (a, b, d) != (0, 0, 0)]
    for o in others:
        pl.semaphore_signal(barrier, inc=1, device_id=at_head(o), device_id_type=MESH)
    for r in (1, 2, 3):
        pl.semaphore_signal(barrier, inc=1, device_id=at_y(r), device_id_type=MESH)
        pl.semaphore_signal(barrier, inc=1, device_id=at_z(r), device_id_type=MESH)

    @pl.when(c != h)
    def _():
        pl.semaphore_signal(barrier, inc=1, device_id=(h, c), device_id_type=MESH)
        pl.semaphore_wait(barrier, 22)

    @pl.when(c == h)
    def _():
        pl.semaphore_wait(barrier, 21)

    def gather(buf, ss, rs):
        def key(o):
            return o[0] * 8 + o[1] * 2 + o[2]

        def forward(o, e):
            rel = ((o[0] + e[0]) % 2, (o[1] - e[1]) % 4, (o[2] + e[2]) % 2)
            block = buf.at[rows(head_of(o)), :]
            send(block, block, ss.at[key(rel)], rs.at[key(rel)], at_head(e))

        def wait(o):
            block = buf.at[rows(head_of(o)), :]
            landed(block, ss.at[key(o)], rs.at[key(o)])

        def begin():
            for e in ((1, 0, 0), (0, 1, 0), (0, 3, 0), (0, 2, 0), (0, 0, 1)):
                forward((0, 0, 0), e)

        events = (
            ((1, 0), ((0, 1, 0), (0, 3, 0), (0, 0, 1))),
            ((0, 1), ((0, 0, 1),)),
            ((0, 3), ((0, 0, 1),)),
            ((0, 2), ((1, 0, 0), (0, 0, 1))),
            ((1, 1), ((0, 0, 1),)),
            ((1, 3), ((0, 0, 1),)),
            ((1, 2), ((0, 0, 1),)),
        )

        def finish(consume):
            def take(chip):
                wait((chip[0], chip[1], 1))
                consume(head_of((chip[0], chip[1], 0)) // 2)

            last = (0, 0)
            for chip, targets in events:
                wait((chip[0], chip[1], 0))
                for e in targets:
                    forward((chip[0], chip[1], 0), e)
                take(last)
                last = chip
            take(last)

        return begin, finish

    def scatter(produce, k):
        ss, rs = rs_s.at[k], rs_r.at[k]
        rc, rx, rx2, rz, sb, pt = r_core.at[k], r_x.at[k], r_x2.at[k], r_z.at[k], s_buf.at[k], part.at[k]
        order = ((1, 2), (1, 1), (1, 3), (0, 1), (0, 3), (0, 2), (1, 0), (0, 0))

        def make(i):
            chip = head_of((order[i][0], order[i][1], 0)) // 2
            pt[rows(chip, PAIR), :] = produce(chip).astype(BF16)
            block = pt.at[rows(chip * 2 + 1 - q), :]
            send(block, rc.at[i], ss.at[i], rs.at[i], at_head((0, 0, 1)))

        def settle(i):
            dz, dx = order[i]
            landed(rc.at[i], ss.at[i], rs.at[i])
            total = pt[rows(head_of((dz, dx, 0))), :].astype(F32) + rc[i].astype(F32)
            if (dz, dx) == (1, 2):
                sb[i] = total.astype(BF16)
                send(sb.at[i], rz.at[0], ss.at[8], rs.at[8], at_head((1, 0, 0)))
            elif dx in (1, 3):
                j = (dx // 2) * 2 + dz
                sb[i] = total.astype(BF16)
                send(sb.at[i], rx.at[j], ss.at[9 + j], rs.at[9 + j], at_head((0, dx, 0)))
            elif (dz, dx) == (0, 2):
                landed(rz.at[0], ss.at[8], rs.at[8])
                sb[i] = (total + rz[0].astype(F32)).astype(BF16)
                send(sb.at[i], rx2, ss.at[13], rs.at[13], at_head((0, 2, 0)))
            elif (dz, dx) == (1, 0):
                for j in (1, 3):
                    landed(rx.at[j], ss.at[9 + j], rs.at[9 + j])
                    total = total + rx[j].astype(F32)
                sb[i] = total.astype(BF16)
                send(sb.at[i], rz.at[1], ss.at[14], rs.at[14], at_head((1, 0, 0)))
            else:
                for j in (0, 2):
                    landed(rx.at[j], ss.at[9 + j], rs.at[9 + j])
                    total = total + rx[j].astype(F32)
                landed(rx2, ss.at[13], rs.at[13])
                total = total + rx2[...].astype(F32)
                landed(rz.at[1], ss.at[14], rs.at[14])
                total = total + rz[1].astype(F32)
                return total
            return None

        for i in range(8):
            make(i)
            if i > 0:
                settle(i - 1)
        return settle(7)

    ag_begin, ag_finish = gather(xt, ag_s.at[0], ag_r.at[0])
    ag_begin()
    acc[...] = jnp.zeros_like(acc)
    loads[3].wait()

    def turn(i, carry):
        at = pl.multiple_of(i * 128, 128)
        wot[pl.ds(at, 128), :] = wo[:, pl.ds(at, 128)].T
        return carry

    lax.fori_loop(0, D // 128, turn, 0)
    for cp in loads[:3]:
        cp.wait()

    def project(chip):
        acc[...] += dot_tn(w[rows(chip, PAIR), :], xt[rows(chip, PAIR), :])

    ag_finish(project)
    cos, sin = cos_ref[...], sin_ref[...]
    qt[:, 0:T] = rot(acc[0:128, :], cos, sin).astype(BF16)
    qt[:, T : 2 * T] = rot(acc[128:256, :], cos, sin).astype(BF16)
    kv[4, 0:128, :] = rot(acc[256:384, :], cos, sin).astype(BF16)
    kv[4, 128:256, :] = acc[384:512, :].astype(BF16)

    def kv_out(slot, r):
        return pltpu.make_async_remote_copy(
            src_ref=kv.at[slot], dst_ref=kv.at[4 - r], send_sem=kv_s.at[r], recv_sem=kv_r.at[r],
            device_id=at_y(r), device_id_type=MESH,
        )

    def kv_up():
        return pltpu.make_async_remote_copy(
            src_ref=kv.at[4], dst_ref=kv.at[0], send_sem=kv_s.at[0], recv_sem=kv_r.at[0],
            device_id=at_z(1), device_id_type=MESH,
        )

    @pl.when(zh < 3)
    def _():
        kv_up().start()

    for r in (1, 2, 3):

        @pl.when(y + r < 4)
        def _():
            kv_out(4, r).start()

    @pl.when(zh == 0)
    def _():
        kv[0] = jnp.zeros((256, T), BF16)

    @pl.when(zh > 0)
    def _():
        kv_up().wait_recv()

    for r in (1, 2, 3):

        @pl.when(y + r >= 4)
        def _():
            kv_out(0, r).start()

    lane = lax.broadcasted_iota(jnp.int32, (1, T), 1)
    limit = jnp.minimum(jnp.minimum(pos_ref[...], WINDOW - 1), lane + c * T)
    limit = jnp.concatenate([limit, limit], axis=1)
    token = jnp.concatenate([lane, lane], axis=1)
    base = lax.broadcasted_iota(jnp.int32, (STEP, 2 * T), 0)
    gap = token - base
    neg = jnp.full((STEP, 2 * T), -jnp.inf, F32)

    highest = jnp.full((8, 2 * T), -jnp.inf, F32)
    for slot in (4, 0, 3, 1, 2):
        if slot in (1, 2, 3):
            kv_out(0, 4 - slot).wait_recv()
        s_scr[slot] = dot_tn(kv[slot, 0:128, :], qt[...])

        def mask(i, top, slot=slot):
            at = pl.multiple_of(i * STEP, STEP)
            distance = gap + ((4 - slot) * T - at)
            scores = s_scr[slot, pl.ds(at, STEP), :] * SCALE
            scores = jnp.where((distance >= 0) & (distance <= limit), scores, neg)
            s_scr[slot, pl.ds(at, STEP), :] = scores
            for j in range(0, STEP, 8):
                top = jnp.maximum(top, scores[j : j + 8])
            return top

        highest = lax.fori_loop(0, T // STEP, mask, highest)
    highest = jnp.max(highest, axis=0, keepdims=True)

    def expo(i, total):
        at = pl.multiple_of(i * STEP, STEP)
        slot, at = i // (T // STEP), pl.multiple_of((i % (T // STEP)) * STEP, STEP)
        e = jnp.exp(s_scr[slot, pl.ds(at, STEP), :] - highest)
        p_scr[slot, pl.ds(at, STEP), :] = e
        return total + fold(e)

    total = lax.fori_loop(0, 5 * T // STEP, expo, jnp.zeros((8, 2 * T), F32))
    recip = 1.0 / jnp.sum(total, axis=0, keepdims=True)

    def norm(i, carry):
        slot, at = i // (T // STEP), pl.multiple_of((i % (T // STEP)) * STEP, STEP)
        p = p_scr[slot, pl.ds(at, STEP), :] * recip
        p_scr[slot, pl.ds(at, STEP), :] = p
        wt_scr[slot, pl.ds(at, STEP), :] = p.astype(BF16)
        return carry

    lax.fori_loop(0, 5 * T // STEP, norm, 0)
    out = dot_nn(kv[0, 128:256, :], wt_scr[0])
    for slot in range(1, 5):
        out = out + dot_nn(kv[slot, 128:256, :], wt_scr[slot])
    out = out.astype(BF16)
    att[0:128, :] = out[:, 0:T]
    att[128:256, :] = out[:, T : 2 * T]
    att_all[c] = att[...]

    for r in (1, 2, 3):
        send(att, att_all.at[c], at_s.at[r], at_r.at[r], at_z(r))

    def project_out(chip):
        return dot_nn(wot[rows(chip, PAIR), :], att[...])

    branch[...] = scatter(project_out, 0)
    gain = gain_ref[...]
    scaled = cot_ref[...].astype(F32) * gain
    stat[h] = jnp.zeros((8, T), F32)
    stat[h, 0:1, :] = jnp.sum(branch[...] * branch[...], axis=0, keepdims=True)
    stat[h, 1:2, :] = jnp.sum(scaled * branch[...], axis=0, keepdims=True)
    for i, o in enumerate(others):
        send(stat.at[h], stat.at[h], st_s.at[i], st_r.at[i], at_head(o))

    for r in (1, 2, 3):
        source = ((zh + 4 - r) % 4) * 4 + y
        landed(att_all.at[source], at_s.at[r], at_r.at[r])
    for r in (1, 2, 3):
        for dz in range(4):
            block = att_all.at[((zh + dz) % 4) * 4 + y]
            i = 4 + (r - 1) * 4 + dz
            send(block, block, at_s.at[i], at_r.at[i], at_y(r))

    for i, o in enumerate(others):
        back = head_of((o[0], (4 - o[1]) % 4, o[2]))
        landed(stat.at[back], st_s.at[i], st_r.at[i])
    sums = stat[0]
    for i in range(1, 16):
        sums = sums + stat[i]
    inverse = lax.rsqrt(sums[0:1] / D + EPSILON)
    slopes = inverse * sums[1:2] / D
    normed = branch[...] * inverse
    bg[rows(h), :] = (inverse * (scaled - normed * slopes)).astype(BF16)
    bg_begin, bg_finish = gather(bg, ag_s.at[1], ag_r.at[1])
    bg_begin()
    hidden_ref[...] = (x_ref[...].astype(F32) + normed * gain).astype(BF16)

    def mirror():
        return pltpu.make_async_remote_copy(
            src_ref=bg.at[rows(h), :], dst_ref=bgt.at[rows(c), :], send_sem=pm_s, recv_sem=pm_r,
            device_id=(h, c), device_id_type=MESH,
        )

    def mirrored():
        return pltpu.make_async_remote_copy(
            src_ref=bg.at[rows(h), :], dst_ref=bgt.at[rows(h), :], send_sem=pm_s, recv_sem=pm_r,
            device_id=(h, c), device_id_type=MESH,
        )

    @pl.when(c != h)
    def _():
        mirror().start()

    @pl.when(c == h)
    def _():
        bgt[rows(h), :] = bg[rows(h), :]

    for r in (1, 2, 3):
        for dz in range(4):
            i = (r - 1) * 4 + dz
            send(
                xt.at[rows(dz * 4 + (y + r) % 4), :], xa.at[r - 1, dz], xa_s.at[i], xa_r.at[i], at_y(r)
            )

    acc[0:256, :] = jnp.zeros((256, T), F32)

    def project_back(chip):
        acc[0:256, :] += dot_tn(wot[rows(chip, PAIR), :], bg[rows(chip, PAIR), :])

    bg_finish(project_back)
    ga[:, 0:T] = acc[0:128, :].astype(BF16)
    ga[:, T : 2 * T] = acc[128:256, :].astype(BF16)

    @pl.when(c != h)
    def _():
        mirrored().wait_recv()

    bgt_begin, bgt_finish = gather(bgt, ag_s.at[2], ag_r.at[2])
    bgt_begin()

    inner = jnp.zeros((8, 2 * T), F32)
    for slot in range(5):
        s_scr[slot] = dot_tn(kv[slot, 128:256, :], ga[...])

    def weigh(i, total):
        slot, at = i // (T // STEP), pl.multiple_of((i % (T // STEP)) * STEP, STEP)
        return total + fold(p_scr[slot, pl.ds(at, STEP), :] * s_scr[slot, pl.ds(at, STEP), :])

    inner = jnp.sum(lax.fori_loop(0, 5 * T // STEP, weigh, inner), axis=0, keepdims=True)

    ds = acc_ds = None
    dq = None
    own_kv = None
    for slot in (1, 2, 3, 0, 4):

        def grad(i, carry, slot=slot):
            at = pl.multiple_of(i * STEP, STEP)
            p = p_scr[slot, pl.ds(at, STEP), :]
            d = p * (s_scr[slot, pl.ds(at, STEP), :] - inner)
            part[1, pl.ds(pl.multiple_of(slot * 512 + at, STEP), STEP), :] = d[:, 0:T].astype(BF16)
            part[1, pl.ds(pl.multiple_of(slot * 512 + 256 + at, STEP), STEP), :] = d[:, T : 2 * T].astype(BF16)
            return carry

        lax.fori_loop(0, T // STEP, grad, 0)
        d0 = part[1, slot * 512 : slot * 512 + 256, :]
        d1 = part[1, slot * 512 + 256 : slot * 512 + 512, :]
        dk = (dot_nt(qt[:, 0:T], d0) + dot_nt(qt[:, T : 2 * T], d1)) * SCALE
        dv = dot_nt(ga[...], wt_scr[slot])
        if slot in (1, 2, 3):
            halo_out[slot - 1, 0:128, :] = dk.astype(BF16)
            halo_out[slot - 1, 128:256, :] = dv.astype(BF16)
            send(
                halo_out.at[slot - 1], halo_in.at[slot - 1], ha_s.at[slot], ha_r.at[slot], at_y(slot)
            )
        else:
            i = 0 if slot == 0 else 1
            halo_prev[i, 0:128, :] = dk
            halo_prev[i, 128:256, :] = dv
        k_slot = kv[slot, 0:128, :]
        part0, part1 = dot_nn(k_slot, d0), dot_nn(k_slot, d1)
        if dq is None:
            acc[0:128, :] = part0
            acc[128:256, :] = part1
            dq = True
        else:
            acc[0:128, :] += part0
            acc[128:256, :] += part1

    g_all[0, 0:128, :] = rot(acc[0:128, :] * SCALE, cos, -sin).astype(BF16)
    g_all[0, 128:256, :] = rot(acc[128:256, :] * SCALE, cos, -sin).astype(BF16)
    for r in (1, 2, 3):
        send(
            g_all.at[0, 0:256, :], g_all.at[r, 0:256, :], g_s.at[r - 1], g_r.at[r - 1], at_y(r)
        )

    for r in (1, 2, 3):
        landed(halo_in.at[r - 1], ha_s.at[r], ha_r.at[r])
        value = halo_in[r - 1].astype(F32)
        back = (y >= r).astype(F32)
        halo_prev[0] += value * back
        halo_prev[1] += value * (1.0 - back)
    halo_z[0] = halo_prev[0].astype(BF16)

    def down():
        return pltpu.make_async_remote_copy(
            src_ref=halo_z.at[0], dst_ref=halo_z.at[1], send_sem=ha_s.at[0], recv_sem=ha_r.at[0],
            device_id=at_z(3), device_id_type=MESH,
        )

    @pl.when(zh > 0)
    def _():
        down().start()

    @pl.when(zh < 3)
    def _():
        down().wait_recv()
        halo_prev[1] += halo_z[1].astype(F32)

    g_all[0, 256:384, :] = rot(halo_prev[1, 0:128, :], cos, -sin).astype(BF16)
    g_all[0, 384:512, :] = halo_prev[1, 128:256, :].astype(BF16)
    for r in (1, 2, 3):
        send(
            g_all.at[0, 256:512, :], g_all.at[r, 256:512, :], g_s.at[r + 2], g_r.at[r + 2], at_y(r)
        )

    for r in (1, 2, 3):
        for dz in range(4):
            i = (r - 1) * 4 + dz
            landed(xa.at[r - 1, dz], xa_s.at[i], xa_r.at[i])

    def weight_grads(k):
        lo = k * 256
        for r in (1, 2, 3):
            i = r - 1 + 3 * k
            landed(g_all.at[r, lo : lo + 256, :], g_s.at[i], g_r.at[i])
        result = None
        for dz in (1, 2, 3, 0):
            z = (zh + dz) % 4
            total = dot_nt(xt[rows(z * 4 + y), :], g_all[0, lo : lo + 256, :])
            for r in (1, 2, 3):
                total = total + dot_nt(xa[r - 1, z], g_all[r, lo : lo + 256, :])
            if dz == 0:
                result = total
            else:
                i = k * 3 + dz - 1
                dw_out[i] = total.astype(BF16)
                send(dw_out.at[i], dw_in.at[i], dw_s.at[i], dw_r.at[i], at_z(dz))
        return result

    dwq_ref[...] = weight_grads(0)

    def input_terms(chip):
        return dot_nn(w[rows(chip, PAIR), :], g_all[0])

    dkv = weight_grads(1)
    dwk_ref[...] = dkv[:, 0:128]
    dwv_ref[...] = dkv[:, 128:256]
    gin_ref[...] = (cot_ref[...].astype(F32) + scatter(input_terms, 1)).astype(BF16)

    for r in (1, 2, 3):
        for dz in range(4):
            block = att_all.at[((zh + dz) % 4) * 4 + (y + 4 - r) % 4]
            i = 4 + (r - 1) * 4 + dz
            landed(block, at_s.at[i], at_r.at[i])
    dwo_ref[...] = jnp.zeros_like(dwo_ref)

    def out_grad(chip):
        for j in range(2):
            dwo_ref[...] += dot_nt(bgt[rows(chip * 2 + j), :], att_all[chip * 2 + j])

    bgt_finish(out_grad)

    for dz in (1, 2, 3):
        landed(dw_in.at[dz - 1], dw_s.at[dz - 1], dw_r.at[dz - 1])
        dwq_ref[...] += dw_in[dz - 1].astype(F32)
    for dz in (1, 2, 3):
        landed(dw_in.at[dz + 2], dw_s.at[dz + 2], dw_r.at[dz + 2])
        value = dw_in[dz + 2].astype(F32)
        dwk_ref[...] += value[:, 0:128]
        dwv_ref[...] += value[:, 128:256]

    for copy in pending:
        copy.wait_send()
    for r in (1, 2, 3):
        kv_out(0, r).wait_send()

    @pl.when(zh < 3)
    def _():
        kv_up().wait_send()

    @pl.when(zh > 0)
    def _():
        down().wait_send()

    @pl.when(c != h)
    def _():
        mirror().wait_send()


def local(inputs, positions, w_query, w_key, w_value, w_out, post_gain, cotangent):
    half = HD // 2
    frequency = jnp.exp(jnp.arange(half, dtype=F32) * (-2.0 * math.log(ROPE_BASE) / HD))
    angles = frequency[:, None] * positions.astype(F32)[None, :]
    vmem = pl.BlockSpec(memory_space=pltpu.VMEM)
    hbm = pl.BlockSpec(memory_space=pl.ANY)
    dma = pltpu.SemaphoreType.DMA
    scratch = [
        pltpu.VMEM((D, 512), BF16),
        pltpu.VMEM((256, D), BF16),
        pltpu.VMEM((D, 256), BF16),
        pltpu.VMEM((D, T), BF16),
        pltpu.VMEM((3, 4, BLK, T), BF16),
        pltpu.VMEM((2, D, T), BF16),
        pltpu.VMEM((D, T), BF16),
        pltpu.VMEM((D, T), BF16),
        pltpu.VMEM((16, 256, T), BF16),
        pltpu.VMEM((256, T), BF16),
        pltpu.VMEM((128, 2 * T), BF16),
        pltpu.VMEM((128, 2 * T), BF16),
        pltpu.VMEM((5, 256, T), BF16),
        pltpu.VMEM((5, T, 2 * T), F32),
        pltpu.VMEM((5, T, 2 * T), F32),
        pltpu.VMEM((5, T, 2 * T), BF16),
        pltpu.VMEM((4, 512, T), BF16),
        pltpu.VMEM((512, T), F32),
        pltpu.VMEM((2, 8, BLK, T), BF16),
        pltpu.VMEM((2, 4, BLK, T), BF16),
        pltpu.VMEM((2, BLK, T), BF16),
        pltpu.VMEM((2, 2, BLK, T), BF16),
        pltpu.VMEM((2, 8, BLK, T), BF16),
        pltpu.VMEM((BLK, T), F32),
        pltpu.VMEM((16, 8, T), F32),
        pltpu.VMEM((3, 256, T), BF16),
        pltpu.VMEM((3, 256, T), BF16),
        pltpu.VMEM((2, 256, T), F32),
        pltpu.VMEM((2, 256, T), BF16),
        pltpu.VMEM((6, BLK, T), BF16),
        pltpu.VMEM((6, BLK, T), BF16),
        dma((4,)),
        dma((3, 16)), dma((3, 16)),
        dma((2, 15)), dma((2, 15)),
        dma((15,)), dma((15,)),
        dma((4,)), dma((4,)),
        dma((12,)), dma((12,)),
        dma((16,)), dma((16,)),
        dma, dma,
        dma((4,)), dma((4,)),
        dma((6,)), dma((6,)),
        dma((6,)), dma((6,)),
    ]
    shapes = (
        jax.ShapeDtypeStruct((BLK, T), BF16),
        jax.ShapeDtypeStruct((BLK, T), BF16),
        jax.ShapeDtypeStruct((BLK, 256), F32),
        jax.ShapeDtypeStruct((BLK, 128), F32),
        jax.ShapeDtypeStruct((BLK, 128), F32),
        jax.ShapeDtypeStruct((BLK, 256), F32),
    )
    hidden, gin, dwq, dwk, dwv, dwo = pl.pallas_call(
        kernel,
        out_shape=shapes,
        in_specs=[vmem] * 6 + [hbm] * 4,
        out_specs=(vmem,) * 6,
        scratch_shapes=scratch,
        compiler_params=pltpu.CompilerParams(
            collective_id=0, has_side_effects=True, vmem_limit_bytes=60 * 1024 * 1024
        ),
        name="layer",
    )(
        inputs.T, cotangent.T, positions[None, :], jnp.cos(angles), jnp.sin(angles),
        post_gain.astype(F32)[:, None], w_query, w_key, w_value, w_out,
    )
    return hidden.T, gin.T, dwq, dwk, dwv, dwo.T


def solution(mesh):
    in_specs = (
        P("ctx", "head"), P("ctx"), P(None, "head"), P(None, "head"),
        P(None, "head"), P("head", None), P("head"), P("ctx", "head"),
    )
    out_specs = (P("ctx", "head"),) * 5 + (P("head", "ctx"),)
    return jax.shard_map(local, mesh=mesh, in_specs=in_specs, out_specs=out_specs, check_vma=False)
```

```python
import functools
import math

import jax
import jax.numpy as jnp
import numpy as np
from jax import lax
from jax.experimental import pallas as pl
from jax.experimental.pallas import tpu as pltpu
from jax.sharding import PartitionSpec as P

D = 5376
HEADS = 32
WINDOW = 1024
EPSILON = 1e-06
ROPE_BASE = 10000.0
HD = 128
T = 256
BLK = 336
PAIR = 672
MESH = pl.DeviceIdType.MESH
F32 = jnp.float32
BF16 = jnp.bfloat16
SCALE = (D // HEADS) ** (-0.5)
STEP = 32


def dot_nn(a, b):
    return lax.dot_general(a, b, (((1,), (0,)), ((), ())), preferred_element_type=F32)


def dot_nt(a, b):
    return lax.dot_general(a, b, (((1,), (1,)), ((), ())), preferred_element_type=F32)


def dot_tn(a, b):
    return lax.dot_general(a, b, (((0,), (0,)), ((), ())), preferred_element_type=F32)


def rot(v, cos, sin):
    half = HD // 2
    a, b = v[:half], v[half:]
    return jnp.concatenate([a * cos - b * sin, b * cos + a * sin], axis=0)


def fold(v):
    total = v[0:8]
    for i in range(8, v.shape[0], 8):
        total = total + v[i : i + 8]
    return total


def kernel(
    x_ref, cot_ref, pos_ref, gain_ref, freq_ref, wq_hbm, wk_hbm, wv_hbm, wo_hbm,
    hidden_ref, gin_ref, dwq_ref, dwk_ref, dwv_ref, dwo_ref,
    w, wo, wot, xt, xa, part, bg, bgt, att_all, att, qt, ga, kv, s_scr, p_scr, wt_scr, g_all,
    acc, r_core, r_x, r_x2, r_z, s_buf, branch, stat, halo_out, halo_in, halo_prev, halo_z, dw_out, dw_in,
    trig, gain_t, scaled_t,
    ds_scr,
    load_sem, ag_s, ag_r, rs_s, rs_r, st_s, st_r, kv_s, kv_r, xa_s, xa_r, at_s, at_r, pm_s, pm_r,
    ha_s, ha_r, g_s, g_r, dw_s, dw_r,
):
    c = lax.axis_index("ctx")
    h = lax.axis_index("head")
    zh, y = c // 4, c % 4
    zl, x, q = h // 8, (h // 2) % 4, h % 2

    def head_of(o):
        return ((zl + o[0]) % 2) * 8 + ((x + o[1]) % 4) * 2 + (q + o[2]) % 2

    def at_head(o):
        return (c, head_of(o))

    def at_y(r):
        return (zh * 4 + (y + r) % 4, h)

    def at_z(r):
        return (((zh + r) % 4) * 4 + y, h)

    def rows(index, size=BLK):
        return pl.ds(pl.multiple_of(index * size, 16), size)

    pending = []
    tail = []

    def send(src, dst, sems, k, device):
        copy = pltpu.make_async_remote_copy(
            src_ref=src, dst_ref=dst, send_sem=sems[0].at[k], recv_sem=sems[1].at[k],
            device_id=device, device_id_type=MESH,
        )
        copy.start()
        pending.append(copy)

    def landed(dst, sems, k):
        pltpu.make_async_remote_copy(
            src_ref=dst, dst_ref=dst, send_sem=sems[0].at[k], recv_sem=sems[1].at[k],
            device_id=at_y(1), device_id_type=MESH,
        ).wait_recv()


    loads = []
    for i, (src, dst) in enumerate(
        (
            (wq_hbm, w.at[:, 0:256]),
            (wk_hbm, w.at[:, 256:384]),
            (wv_hbm, w.at[:, 384:512]),
            (wo_hbm, wo),
        )
    ):
        cp = pltpu.make_async_copy(src, dst, load_sem.at[i])
        cp.start()
        loads.append(cp)
    xt[rows(h), :] = x_ref[...]

    barrier = pltpu.get_barrier_semaphore()
    others = [(a, b, d) for a in (0, 1) for b in range(4) for d in (0, 1) if (a, b, d) != (0, 0, 0)]
    for o in others:
        pl.semaphore_signal(barrier, inc=1, device_id=at_head(o), device_id_type=MESH)
    for r in (1, 2, 3):
        pl.semaphore_signal(barrier, inc=1, device_id=at_y(r), device_id_type=MESH)
        pl.semaphore_signal(barrier, inc=1, device_id=at_z(r), device_id_type=MESH)

    @pl.when(c != h)
    def _():
        pl.semaphore_signal(barrier, inc=1, device_id=(h, c), device_id_type=MESH)
        pl.semaphore_wait(barrier, 22)

    @pl.when(c == h)
    def _():
        pl.semaphore_wait(barrier, 21)

    def gather(buf, sems):
        def key(o):
            return o[0] * 8 + o[1] * 2 + o[2]

        def forward(o, e):
            rel = ((o[0] + e[0]) % 2, (o[1] - e[1]) % 4, (o[2] + e[2]) % 2)
            block = buf.at[rows(head_of(o)), :]
            send(block, block, sems, key(rel), at_head(e))

        def wait(o):
            block = buf.at[rows(head_of(o)), :]
            landed(block, sems, key(o))

        def begin():
            for e in ((1, 0, 0), (0, 1, 0), (0, 3, 0), (0, 2, 0), (0, 0, 1)):
                forward((0, 0, 0), e)

        events = (
            ((1, 0), ((0, 1, 0), (0, 3, 0), (0, 0, 1))),
            ((0, 1), ((0, 0, 1),)),
            ((0, 3), ((0, 0, 1),)),
            ((0, 2), ((1, 0, 0), (0, 0, 1))),
            ((1, 1), ((0, 0, 1),)),
            ((1, 3), ((0, 0, 1),)),
            ((1, 2), ((0, 0, 1),)),
        )

        def relay(chip, targets):
            wait((chip[0], chip[1], 0))
            for e in targets:
                forward((chip[0], chip[1], 0), e)

        def take(chip, consume):
            wait((chip[0], chip[1], 1))
            consume(head_of((chip[0], chip[1], 0)) // 2)

        def finish(consume):
            last = (0, 0)
            for chip, targets in events:
                relay(chip, targets)
                take(last, consume)
                last = chip
            take(last, consume)

        def relays(first, end):
            for chip, targets in events[first:end]:
                relay(chip, targets)

        def takes(consume):
            for chip in ((0, 0),) + tuple(chip for chip, _ in events):
                take(chip, consume)

        return begin, finish, relays, takes

    def scatter(produce, k):
        sems = (rs_s.at[k], rs_r.at[k], (1, k))
        rc, rx, rx2, rz, sb, pt = r_core.at[k], r_x.at[k], r_x2.at[k], r_z.at[k], s_buf.at[k], part.at[k]
        order = ((1, 2), (1, 1), (1, 3), (0, 1), (0, 3), (0, 2), (1, 0), (0, 0))

        def make(i):
            chip = head_of((order[i][0], order[i][1], 0)) // 2
            pt[rows(chip, PAIR), :] = produce(chip).astype(BF16)
            block = pt.at[rows(chip * 2 + 1 - q), :]
            send(block, rc.at[i], sems, i, at_head((0, 0, 1)))

        def settle(i):
            dz, dx = order[i]
            landed(rc.at[i], sems, i)
            total = pt[rows(head_of((dz, dx, 0))), :].astype(F32) + rc[i].astype(F32)
            if (dz, dx) == (1, 2):
                sb[i] = total.astype(BF16)
                send(sb.at[i], rz.at[0], sems, 8, at_head((1, 0, 0)))
            elif dx in (1, 3):
                j = (dx // 2) * 2 + dz
                sb[i] = total.astype(BF16)
                send(sb.at[i], rx.at[j], sems, 9 + j, at_head((0, dx, 0)))
            elif (dz, dx) == (0, 2):
                landed(rz.at[0], sems, 8)
                sb[i] = (total + rz[0].astype(F32)).astype(BF16)
                send(sb.at[i], rx2, sems, 13, at_head((0, 2, 0)))
            elif (dz, dx) == (1, 0):
                for j in (1, 3):
                    landed(rx.at[j], sems, 9 + j)
                    total = total + rx[j].astype(F32)
                sb[i] = total.astype(BF16)
                send(sb.at[i], rz.at[1], sems, 14, at_head((1, 0, 0)))
            else:
                for j in (0, 2):
                    landed(rx.at[j], sems, 9 + j)
                    total = total + rx[j].astype(F32)
                landed(rx2, sems, 13)
                total = total + rx2[...].astype(F32)
                landed(rz.at[1], sems, 14)
                total = total + rz[1].astype(F32)
                return total
            return None

        def first():
            for i in range(8):
                make(i)
                if 0 < i < 6:
                    settle(i - 1)

        def second():
            settle(5)
            settle(6)
            return settle(7)

        return first, second

    ag_begin, ag_finish, _, _ = gather(xt, (ag_s.at[0], ag_r.at[0], (0, 0)))
    ag_begin()
    acc[...] = jnp.zeros_like(acc)
    loads[3].wait()

    def turn(i, carry):
        at = pl.multiple_of(i * 128, 128)
        wot[pl.ds(at, 128), :] = wo[:, pl.ds(at, 128)].T
        return carry

    lax.fori_loop(0, D // 128, turn, 0)
    angles = freq_ref[...] * pos_ref[...].astype(F32)
    trig[0] = jnp.cos(angles)
    trig[1] = jnp.sin(angles)
    gain_t[...] = dot_tn(gain_ref[...].reshape(1, BLK), jnp.ones((1, T), BF16))
    scaled_t[...] = cot_ref[...].astype(F32) * gain_t[...]
    for cp in loads[:3]:
        cp.wait()

    def project(chip):
        acc[...] += dot_tn(w[rows(chip, PAIR), :], xt[rows(chip, PAIR), :])

    ag_finish(project)
    cos, sin = trig[0], trig[1]
    qt[:, 0:T] = rot(acc[0:128, :], cos, sin).astype(BF16)
    qt[:, T : 2 * T] = rot(acc[128:256, :], cos, sin).astype(BF16)
    kv[4, 0:128, :] = rot(acc[256:384, :], cos, sin).astype(BF16)
    kv[4, 128:256, :] = acc[384:512, :].astype(BF16)

    def kv_out(slot, r):
        return pltpu.make_async_remote_copy(
            src_ref=kv.at[slot], dst_ref=kv.at[4 - r], send_sem=kv_s.at[r], recv_sem=kv_r.at[r],
            device_id=at_y(r), device_id_type=MESH,
        )

    def kv_up():
        return pltpu.make_async_remote_copy(
            src_ref=kv.at[4], dst_ref=kv.at[0], send_sem=kv_s.at[0], recv_sem=kv_r.at[0],
            device_id=at_z(1), device_id_type=MESH,
        )

    @pl.when(zh < 3)
    def _():
        kv_up().start()

    for r in (1, 2, 3):

        @pl.when(y + r < 4)
        def _():
            kv_out(4, r).start()

    @pl.when(zh == 0)
    def _():
        kv[0] = jnp.zeros((256, T), BF16)

    @pl.when(zh > 0)
    def _():
        kv_up().wait_recv()

    for r in (1, 2, 3):

        @pl.when(y + r >= 4)
        def _():
            kv_out(0, r).start()

    def kv_sent():
        for r in (1, 2, 3):
            kv_out(0, r).wait_send()

        @pl.when(zh < 3)
        def _():
            kv_up().wait_send()

    tail.append(kv_sent)

    lane = lax.broadcasted_iota(jnp.int32, (1, T), 1)
    limit = jnp.minimum(jnp.minimum(pos_ref[...], WINDOW - 1), lane + c * T)
    limit = jnp.concatenate([limit, limit], axis=1)
    token = jnp.concatenate([lane, lane], axis=1)
    base = lax.broadcasted_iota(jnp.int32, (STEP, 2 * T), 0)
    gap = token - base
    neg = jnp.full((STEP, 2 * T), -jnp.inf, F32)

    highest = jnp.full((8, 2 * T), -jnp.inf, F32)
    for slot in (4, 0, 3, 1, 2):
        if slot in (1, 2, 3):
            kv_out(0, 4 - slot).wait_recv()
        s_scr[slot] = dot_tn(kv[slot, 0:128, :], qt[...])

        def mask(i, top, slot=slot):
            at = pl.multiple_of(i * STEP, STEP)
            distance = gap + ((4 - slot) * T - at)
            scores = s_scr[slot, pl.ds(at, STEP), :] * SCALE
            scores = jnp.where((distance >= 0) & (distance <= limit), scores, neg)
            s_scr[slot, pl.ds(at, STEP), :] = scores
            for j in range(0, STEP, 8):
                top = jnp.maximum(top, scores[j : j + 8])
            return top

        highest = lax.fori_loop(0, T // STEP, mask, highest)
    highest = jnp.max(highest, axis=0, keepdims=True)

    for r in (1, 2, 3):
        for j in range(2):
            dz = q * 2 + j
            send(
                xt.at[rows(dz * 4 + (y + r) % 4), :], xa.at[r - 1, dz], (xa_s, xa_r, 4), (r - 1) * 2 + j, at_y(r)
            )

    def expo(i, total):
        at = pl.multiple_of(i * STEP, STEP)
        slot, at = i // (T // STEP), pl.multiple_of((i % (T // STEP)) * STEP, STEP)
        e = jnp.exp(s_scr[slot, pl.ds(at, STEP), :] - highest)
        p_scr[slot, pl.ds(at, STEP), :] = e
        return total + fold(e)

    total = lax.fori_loop(0, 5 * T // STEP, expo, jnp.zeros((8, 2 * T), F32))
    recip = 1.0 / jnp.sum(total, axis=0, keepdims=True)

    def norm(i, carry):
        slot, at = i // (T // STEP), pl.multiple_of((i % (T // STEP)) * STEP, STEP)
        wt_scr[slot, pl.ds(at, STEP), :] = (p_scr[slot, pl.ds(at, STEP), :] * recip).astype(BF16)
        return carry

    lax.fori_loop(0, 5 * T // STEP, norm, 0)
    out = dot_nn(kv[0, 128:256, :], wt_scr[0])
    for slot in range(1, 5):
        out = out + dot_nn(kv[slot, 128:256, :], wt_scr[slot])
    out = out.astype(BF16)
    att[0:128, :] = out[:, 0:T]
    att[128:256, :] = out[:, T : 2 * T]
    att_all[c] = att[...]

    def project_out(chip):
        return dot_nn(wot[rows(chip, PAIR), :], att[...])

    out_first, out_second = scatter(project_out, 0)
    out_first()
    for r in (1, 2, 3):
        send(att, att_all.at[c], (at_s, at_r, 2), r, at_z(r))
    branch[...] = out_second()
    gain = gain_t[...]
    scaled = scaled_t[...]
    stat[h] = jnp.zeros((8, T), F32)
    stat[h, 0:1, :] = jnp.sum(branch[...] * branch[...], axis=0, keepdims=True)
    stat[h, 1:2, :] = jnp.sum(scaled * branch[...], axis=0, keepdims=True)
    for i, o in enumerate(others):
        send(stat.at[h], stat.at[h], (st_s, st_r, 3), i, at_head(o))

    for i, o in enumerate(others):
        back = head_of((o[0], (4 - o[1]) % 4, o[2]))
        landed(stat.at[back], (st_s, st_r, 3), i)
    sums = stat[0]
    for i in range(1, 16):
        sums = sums + stat[i]
    inverse = lax.rsqrt(sums[0:1] / D + EPSILON)
    slopes = inverse * sums[1:2] / D
    normed = branch[...] * inverse
    bg[rows(h), :] = (inverse * (scaled - normed * slopes)).astype(BF16)
    bg_begin, bg_finish, _, _ = gather(bg, (ag_s.at[1], ag_r.at[1], (0, 1)))
    bg_begin()
    for r in (1, 2, 3):
        source = ((zh + 4 - r) % 4) * 4 + y
        landed(att_all.at[source], (at_s, at_r, 2), r)
    for r in (1, 2, 3):
        for dz in range(4):
            block = att_all.at[((zh + dz) % 4) * 4 + y]
            i = 4 + (r - 1) * 4 + dz
            send(block, block, (at_s, at_r, 2), i, at_y(r))
    hidden_ref[...] = (x_ref[...].astype(F32) + normed * gain).astype(BF16)

    def mirror():
        return pltpu.make_async_remote_copy(
            src_ref=bg.at[rows(h), :], dst_ref=bgt.at[rows(c), :], send_sem=pm_s, recv_sem=pm_r,
            device_id=(h, c), device_id_type=MESH,
        )

    def mirrored():
        return pltpu.make_async_remote_copy(
            src_ref=bg.at[rows(h), :], dst_ref=bgt.at[rows(h), :], send_sem=pm_s, recv_sem=pm_r,
            device_id=(h, c), device_id_type=MESH,
        )

    @pl.when(c != h)
    def _():
        mirror().start()

    def mirror_sent():
        @pl.when(c != h)
        def _():
            mirror().wait_send()

    tail.append(mirror_sent)

    @pl.when(c == h)
    def _():
        bgt[rows(h), :] = bg[rows(h), :]

    acc[0:256, :] = jnp.zeros((256, T), F32)

    def project_back(chip):
        acc[0:256, :] += dot_tn(wot[rows(chip, PAIR), :], bg[rows(chip, PAIR), :])

    bg_finish(project_back)
    ga[:, 0:T] = acc[0:128, :].astype(BF16)
    ga[:, T : 2 * T] = acc[128:256, :].astype(BF16)

    @pl.when(c != h)
    def _():
        mirrored().wait_recv()

    bgt_begin, _, bgt_relays, bgt_takes = gather(bgt, (ag_s.at[2], ag_r.at[2], (0, 2)))
    bgt_begin()
    for r in (1, 2, 3):
        for j in range(2):
            block = xa.at[r - 1, q * 2 + j]
            landed(block, (xa_s, xa_r, 4), (r - 1) * 2 + j)
            send(block, block, (xa_s, xa_r, 4), 6 + (r - 1) * 2 + j, at_head((0, 0, 1)))

    inner = jnp.zeros((8, 2 * T), F32)
    for slot in range(5):
        s_scr[slot] = dot_tn(kv[slot, 128:256, :], ga[...])

    def weigh(i, total):
        slot, at = i // (T // STEP), pl.multiple_of((i % (T // STEP)) * STEP, STEP)
        return total + fold(p_scr[slot, pl.ds(at, STEP), :] * s_scr[slot, pl.ds(at, STEP), :])

    inner = jnp.sum(lax.fori_loop(0, 5 * T // STEP, weigh, inner), axis=0, keepdims=True) * recip

    def grad(i, carry):
        slot, at = i // (T // STEP), pl.multiple_of((i % (T // STEP)) * STEP, STEP)
        p = p_scr[slot, pl.ds(at, STEP), :] * recip
        ds_scr[slot, pl.ds(at, STEP), :] = (p * (s_scr[slot, pl.ds(at, STEP), :] - inner)).astype(BF16)
        return carry

    lax.fori_loop(0, 5 * T // STEP, grad, 0)
    dq = dot_nn(kv[0, 0:128, :], ds_scr[0])
    for slot in range(1, 5):
        dq = dq + dot_nn(kv[slot, 0:128, :], ds_scr[slot])
    dq = dq * SCALE
    g_all[0, 0:128, :] = rot(dq[:, 0:T], cos, -sin).astype(BF16)
    g_all[0, 128:256, :] = rot(dq[:, T : 2 * T], cos, -sin).astype(BF16)
    for r in (1, 2, 3):
        send(
            g_all.at[0, 0:256, :], g_all.at[r, 0:256, :], (g_s, g_r, 6), r - 1, at_y(r)
        )

    for slot in (1, 2, 3, 0, 4):
        dk = dot_nt(qt[...], ds_scr[slot]) * SCALE
        dv = dot_nt(ga[...], wt_scr[slot])
        if slot in (1, 2, 3):
            halo_out[slot - 1, 0:128, :] = dk.astype(BF16)
            halo_out[slot - 1, 128:256, :] = dv.astype(BF16)
            send(
                halo_out.at[slot - 1], halo_in.at[slot - 1], (ha_s, ha_r, 5), slot, at_y(slot)
            )
        else:
            i = 0 if slot == 0 else 1
            halo_prev[i, 0:128, :] = dk
            halo_prev[i, 128:256, :] = dv
    bgt_relays(0, 4)

    for r in (1, 2, 3):
        landed(halo_in.at[r - 1], (ha_s, ha_r, 5), r)
        value = halo_in[r - 1].astype(F32)
        back = (y >= r).astype(F32)
        halo_prev[0] += value * back
        halo_prev[1] += value * (1.0 - back)
    halo_z[0] = halo_prev[0].astype(BF16)

    def down():
        return pltpu.make_async_remote_copy(
            src_ref=halo_z.at[0], dst_ref=halo_z.at[1], send_sem=ha_s.at[0], recv_sem=ha_r.at[0],
            device_id=at_z(3), device_id_type=MESH,
        )

    @pl.when(zh > 0)
    def _():
        down().start()

    def down_sent():
        @pl.when(zh > 0)
        def _():
            down().wait_send()

    tail.append(down_sent)

    for r in (1, 2, 3):
        for j in range(2):
            landed(xa.at[r - 1, (1 - q) * 2 + j], (xa_s, xa_r, 4), 6 + (r - 1) * 2 + j)

    def weight_grads(k):
        lo = k * 256
        for r in (1, 2, 3):
            i = r - 1 + 3 * k
            landed(g_all.at[r, lo : lo + 256, :], (g_s, g_r, 6), i)
        result = None
        for dz in (1, 2, 3, 0):
            z = (zh + dz) % 4
            total = dot_nt(xt[rows(z * 4 + y), :], g_all[0, lo : lo + 256, :])
            for r in (1, 2, 3):
                total = total + dot_nt(xa[r - 1, z], g_all[r, lo : lo + 256, :])
            if dz == 0:
                result = total
            else:
                i = k * 3 + dz - 1
                dw_out[i] = total.astype(BF16)
                send(dw_out.at[i], dw_in.at[i], (dw_s, dw_r, 7), i, at_z(dz))
        return result

    dwq_ref[...] = weight_grads(0)
    bgt_relays(4, 7)

    @pl.when(zh < 3)
    def _():
        down().wait_recv()
        halo_prev[1] += halo_z[1].astype(F32)

    g_all[0, 256:384, :] = rot(halo_prev[1, 0:128, :], cos, -sin).astype(BF16)
    g_all[0, 384:512, :] = halo_prev[1, 128:256, :].astype(BF16)
    for r in (1, 2, 3):
        send(
            g_all.at[0, 256:512, :], g_all.at[r, 256:512, :], (g_s, g_r, 6), r + 2, at_y(r)
        )


    def input_terms(chip):
        return dot_nn(w[rows(chip, PAIR), :], g_all[0])

    in_first, in_second = scatter(input_terms, 1)
    in_first()
    dkv = weight_grads(1)
    dwk_ref[...] = dkv[:, 0:128]
    dwv_ref[...] = dkv[:, 128:256]
    gin_ref[...] = (cot_ref[...].astype(F32) + in_second()).astype(BF16)

    for r in (1, 2, 3):
        for dz in range(4):
            block = att_all.at[((zh + dz) % 4) * 4 + (y + 4 - r) % 4]
            i = 4 + (r - 1) * 4 + dz
            landed(block, (at_s, at_r, 2), i)
    dwo_ref[...] = jnp.zeros_like(dwo_ref)

    def out_grad(chip):
        for j in range(2):
            dwo_ref[...] += dot_nt(bgt[rows(chip * 2 + j), :], att_all[chip * 2 + j])

    bgt_takes(out_grad)

    for dz in (1, 2, 3):
        landed(dw_in.at[dz - 1], (dw_s, dw_r, 7), dz - 1)
        dwq_ref[...] += dw_in[dz - 1].astype(F32)
    for dz in (1, 2, 3):
        landed(dw_in.at[dz + 2], (dw_s, dw_r, 7), dz + 2)
        value = dw_in[dz + 2].astype(F32)
        dwk_ref[...] += value[:, 0:128]
        dwv_ref[...] += value[:, 128:256]

    for copy in pending:
        copy.wait_send()
    for wait in tail:
        wait()


def settle(*refs):
    for i in range(6):
        refs[6 + i][...] = refs[i][...]


def local(inputs, positions, w_query, w_key, w_value, w_out, post_gain, cotangent):
    frequency = np.exp(np.arange(HD // 2, dtype=np.float32) * np.float32(-2.0 * math.log(ROPE_BASE) / HD))[:, None]
    vmem = pl.BlockSpec(memory_space=pltpu.VMEM)
    hbm = pl.BlockSpec(memory_space=pl.ANY)
    dma = pltpu.SemaphoreType.DMA
    scratch = [
        pltpu.VMEM((D, 512), BF16),
        pltpu.VMEM((256, D), BF16),
        pltpu.VMEM((D, 256), BF16),
        pltpu.VMEM((D, T), BF16),
        pltpu.VMEM((3, 4, BLK, T), BF16),
        pltpu.VMEM((2, D, T), BF16),
        pltpu.VMEM((D, T), BF16),
        pltpu.VMEM((D, T), BF16),
        pltpu.VMEM((16, 256, T), BF16),
        pltpu.VMEM((256, T), BF16),
        pltpu.VMEM((128, 2 * T), BF16),
        pltpu.VMEM((128, 2 * T), BF16),
        pltpu.VMEM((5, 256, T), BF16),
        pltpu.VMEM((5, T, 2 * T), F32),
        pltpu.VMEM((5, T, 2 * T), F32),
        pltpu.VMEM((5, T, 2 * T), BF16),
        pltpu.VMEM((4, 512, T), BF16),
        pltpu.VMEM((512, T), F32),
        pltpu.VMEM((2, 8, BLK, T), BF16),
        pltpu.VMEM((2, 4, BLK, T), BF16),
        pltpu.VMEM((2, BLK, T), BF16),
        pltpu.VMEM((2, 2, BLK, T), BF16),
        pltpu.VMEM((2, 8, BLK, T), BF16),
        pltpu.VMEM((BLK, T), F32),
        pltpu.VMEM((16, 8, T), F32),
        pltpu.VMEM((3, 256, T), BF16),
        pltpu.VMEM((3, 256, T), BF16),
        pltpu.VMEM((2, 256, T), F32),
        pltpu.VMEM((2, 256, T), BF16),
        pltpu.VMEM((6, BLK, T), BF16),
        pltpu.VMEM((6, BLK, T), BF16),
        pltpu.VMEM((2, HD // 2, T), F32),
        pltpu.VMEM((BLK, T), F32),
        pltpu.VMEM((BLK, T), F32),
        pltpu.VMEM((5, T, 2 * T), BF16),
        dma((4,)),
        dma((3, 16)), dma((3, 16)),
        dma((2, 15)), dma((2, 15)),
        dma((15,)), dma((15,)),
        dma((4,)), dma((4,)),
        dma((12,)), dma((12,)),
        dma((16,)), dma((16,)),
        dma, dma,
        dma((4,)), dma((4,)),
        dma((6,)), dma((6,)),
        dma((6,)), dma((6,)),
    ]
    shapes = (
        jax.ShapeDtypeStruct((BLK, T), BF16),
        jax.ShapeDtypeStruct((BLK, T), BF16),
        jax.ShapeDtypeStruct((BLK, 256), F32),
        jax.ShapeDtypeStruct((BLK, 128), F32),
        jax.ShapeDtypeStruct((BLK, 128), F32),
        jax.ShapeDtypeStruct((BLK, 256), F32),
    )
    results = pl.pallas_call(
        kernel,
        out_shape=shapes,
        in_specs=[vmem] * 5 + [hbm] * 4,
        out_specs=(vmem,) * 6,
        scratch_shapes=scratch,
        compiler_params=pltpu.CompilerParams(
            collective_id=0, has_side_effects=True, vmem_limit_bytes=60 * 1024 * 1024
        ),
        name="layer",
    )(
        inputs.T, cotangent.T, positions[None, :], post_gain, frequency,
        w_query, w_key, w_value, w_out,
    )
    hidden, gin, dwq, dwk, dwv, dwo = pl.pallas_call(
        settle,
        out_shape=shapes,
        in_specs=[vmem] * 6,
        out_specs=(vmem,) * 6,
        name="results",
    )(*results)
    return hidden.T, gin.T, dwq, dwk, dwv, dwo.T


def solution(mesh):
    in_specs = (
        P("ctx", "head"), P("ctx"), P(None, "head"), P(None, "head"),
        P(None, "head"), P("head", None), P("head"), P("ctx", "head"),
    )
    out_specs = (P("ctx", "head"),) * 5 + (P("head", "ctx"),)
    return jax.shard_map(local, mesh=mesh, in_specs=in_specs, out_specs=out_specs, check_vma=False)
```

```python
import functools
import math

import jax
import jax.numpy as jnp
import numpy as np
from jax import lax
from jax.experimental import pallas as pl
from jax.experimental.pallas import tpu as pltpu
from jax.sharding import PartitionSpec as P

D = 5376
HEADS = 32
WINDOW = 1024
EPSILON = 1e-06
ROPE_BASE = 10000.0
HD = 128
T = 256
BLK = 336
PAIR = 672
HALF = 176
MESH = pl.DeviceIdType.MESH
F32 = jnp.float32
BF16 = jnp.bfloat16
SCALE = (D // HEADS) ** (-0.5)
STEP = 32


def dot_nn(a, b):
    return lax.dot_general(a, b, (((1,), (0,)), ((), ())), preferred_element_type=F32)


def dot_nt(a, b):
    return lax.dot_general(a, b, (((1,), (1,)), ((), ())), preferred_element_type=F32)


def dot_tn(a, b):
    return lax.dot_general(a, b, (((0,), (0,)), ((), ())), preferred_element_type=F32)


def rot(v, cos, sin):
    half = HD // 2
    a, b = v[:half], v[half:]
    return jnp.concatenate([a * cos - b * sin, b * cos + a * sin], axis=0)


def fold(v):
    total = v[0:8]
    for i in range(8, v.shape[0], 8):
        total = total + v[i : i + 8]
    return total


def kernel(
    x_ref, cot_ref, pos_ref, gain_ref, freq_ref, wq_hbm, wk_hbm, wv_hbm, wo_hbm,
    hidden_ref, gin_ref, dwq_ref, dwk_ref, dwv_ref, dwo_ref,
    w, wo, wot, xt, xa, part, bg, bgt, att_all, att, qt, ga, kv, s_scr, p_scr, wt_scr, g_all,
    acc, r_core, r_x, r_x2, r_z, s_buf, branch, stat, halo_out, halo_in, halo_prev, halo_z, dw_out, dw_in,
    trig, gain_t, scaled_t,
    ds_scr,
    load_sem, ag_s, ag_r, rs_s, rs_r, st_s, st_r, kv_s, kv_r, xa_s, xa_r, at_s, at_r, pm_s, pm_r,
    ha_s, ha_r, g_s, g_r, dw_s, dw_r,
):
    c = lax.axis_index("ctx")
    h = lax.axis_index("head")
    zh, y = c // 4, c % 4
    zl, x, q = h // 8, (h // 2) % 4, h % 2

    def head_of(o):
        return ((zl + o[0]) % 2) * 8 + ((x + o[1]) % 4) * 2 + (q + o[2]) % 2

    def at_head(o):
        return (c, head_of(o))

    def at_y(r):
        return (zh * 4 + (y + r) % 4, h)

    def at_z(r):
        return (((zh + r) % 4) * 4 + y, h)

    def rows(index, size=BLK):
        return pl.ds(pl.multiple_of(index * size, 16), size)

    pending = []
    tail = []

    def send(src, dst, sems, k, device):
        copy = pltpu.make_async_remote_copy(
            src_ref=src, dst_ref=dst, send_sem=sems[0].at[k], recv_sem=sems[1].at[k],
            device_id=device, device_id_type=MESH,
        )
        copy.start()
        pending.append(copy)

    def landed(dst, sems, k):
        pltpu.make_async_remote_copy(
            src_ref=dst, dst_ref=dst, send_sem=sems[0].at[k], recv_sem=sems[1].at[k],
            device_id=at_y(1), device_id_type=MESH,
        ).wait_recv()


    loads = []
    for i, (src, dst) in enumerate(
        (
            (wq_hbm, w.at[:, 0:256]),
            (wk_hbm, w.at[:, 256:384]),
            (wv_hbm, w.at[:, 384:512]),
            (wo_hbm, wo),
        )
    ):
        cp = pltpu.make_async_copy(src, dst, load_sem.at[i])
        cp.start()
        loads.append(cp)
    xt[rows(h), :] = x_ref[...]

    barrier = pltpu.get_barrier_semaphore()
    others = [(a, b, d) for a in (0, 1) for b in range(4) for d in (0, 1) if (a, b, d) != (0, 0, 0)]
    for o in others:
        pl.semaphore_signal(barrier, inc=1, device_id=at_head(o), device_id_type=MESH)
    for r in (1, 2, 3):
        pl.semaphore_signal(barrier, inc=1, device_id=at_y(r), device_id_type=MESH)
        pl.semaphore_signal(barrier, inc=1, device_id=at_z(r), device_id_type=MESH)

    @pl.when(c != h)
    def _():
        pl.semaphore_signal(barrier, inc=1, device_id=(h, c), device_id_type=MESH)
        pl.semaphore_wait(barrier, 22)

    @pl.when(c == h)
    def _():
        pl.semaphore_wait(barrier, 21)

    def gather(buf, sems):
        def key(o):
            return o[0] * 8 + o[1] * 2 + o[2]

        def forward(o, e):
            rel = ((o[0] + e[0]) % 2, (o[1] - e[1]) % 4, (o[2] + e[2]) % 2)
            block = buf.at[rows(head_of(o)), :]
            send(block, block, sems, key(rel), at_head(e))

        def wait(o):
            block = buf.at[rows(head_of(o)), :]
            landed(block, sems, key(o))

        def begin():
            for e in ((1, 0, 0), (0, 1, 0), (0, 3, 0), (0, 2, 0), (0, 0, 1)):
                forward((0, 0, 0), e)

        events = (
            ((1, 0), ((0, 1, 0), (0, 3, 0), (0, 0, 1))),
            ((0, 1), ((0, 0, 1),)),
            ((0, 3), ((0, 0, 1),)),
            ((0, 2), ((1, 0, 0), (0, 0, 1))),
            ((1, 1), ((0, 0, 1),)),
            ((1, 3), ((0, 0, 1),)),
            ((1, 2), ((0, 0, 1),)),
        )

        def relay(chip, targets):
            wait((chip[0], chip[1], 0))
            for e in targets:
                forward((chip[0], chip[1], 0), e)

        def take(chip, consume):
            wait((chip[0], chip[1], 1))
            consume(head_of((chip[0], chip[1], 0)) // 2)

        def finish(consume):
            last = (0, 0)
            for chip, targets in events:
                relay(chip, targets)
                take(last, consume)
                last = chip
            take(last, consume)

        def relays(first, end):
            for chip, targets in events[first:end]:
                relay(chip, targets)

        def takes(consume):
            for chip in ((0, 0),) + tuple(chip for chip, _ in events):
                take(chip, consume)

        return begin, finish, relays, takes

    def scatter(produce, k):
        sems = (rs_s.at[k], rs_r.at[k], (1, k))
        rc, rx, rx2, rz, sb, pt = r_core.at[k], r_x.at[k], r_x2.at[k], r_z.at[k], s_buf.at[k], part.at[k]
        order = ((1, 2), (1, 1), (1, 3), (0, 1), (0, 3), (0, 2), (1, 0), (0, 0))

        def make(i):
            chip = head_of((order[i][0], order[i][1], 0)) // 2
            pt[rows(chip, PAIR), :] = produce(chip).astype(BF16)
            block = pt.at[rows(chip * 2 + 1 - q), :]
            send(block, rc.at[i], sems, i, at_head((0, 0, 1)))

        def settle(i):
            dz, dx = order[i]
            landed(rc.at[i], sems, i)
            total = pt[rows(head_of((dz, dx, 0))), :].astype(F32) + rc[i].astype(F32)
            if (dz, dx) == (1, 2):
                sb[i] = total.astype(BF16)
                send(sb.at[i], rz.at[0], sems, 8, at_head((1, 0, 0)))
            elif dx in (1, 3):
                j = (dx // 2) * 2 + dz
                sb[i] = total.astype(BF16)
                send(sb.at[i], rx.at[j], sems, 9 + j, at_head((0, dx, 0)))
            elif (dz, dx) == (0, 2):
                landed(rz.at[0], sems, 8)
                sb[i] = (total + rz[0].astype(F32)).astype(BF16)
                send(sb.at[i], rx2, sems, 13, at_head((0, 2, 0)))
            elif (dz, dx) == (1, 0):
                for j in (1, 3):
                    landed(rx.at[j], sems, 9 + j)
                    total = total + rx[j].astype(F32)
                sb[i] = total.astype(BF16)
                send(sb.at[i], rz.at[1], sems, 14, at_head((1, 0, 0)))
            else:
                for j in (0, 2):
                    landed(rx.at[j], sems, 9 + j)
                    total = total + rx[j].astype(F32)
                landed(rx2, sems, 13)
                total = total + rx2[...].astype(F32)
                landed(rz.at[1], sems, 14)
                total = total + rz[1].astype(F32)
                return total
            return None

        def first():
            for i in range(8):
                make(i)
                if 0 < i < 6:
                    settle(i - 1)

        def second():
            settle(5)
            settle(6)
            return settle(7)

        return first, second

    ag_begin, ag_finish, _, _ = gather(xt, (ag_s.at[0], ag_r.at[0], (0, 0)))
    ag_begin()
    acc[...] = jnp.zeros_like(acc)
    loads[3].wait()

    def turn(i, carry):
        at = pl.multiple_of(i * 128, 128)
        wot[pl.ds(at, 128), :] = wo[:, pl.ds(at, 128)].T
        return carry

    lax.fori_loop(0, D // 128, turn, 0)
    angles = freq_ref[...] * pos_ref[...].astype(F32)
    trig[0] = jnp.cos(angles)
    trig[1] = jnp.sin(angles)
    gain_t[...] = dot_tn(gain_ref[...].reshape(1, BLK), jnp.ones((1, T), BF16))
    scaled_t[...] = cot_ref[...].astype(F32) * gain_t[...]
    for cp in loads[:3]:
        cp.wait()

    def project(chip):
        acc[...] += dot_tn(w[rows(chip, PAIR), :], xt[rows(chip, PAIR), :])

    ag_finish(project)
    cos, sin = trig[0], trig[1]
    qt[:, 0:T] = rot(acc[0:128, :], cos, sin).astype(BF16)
    qt[:, T : 2 * T] = rot(acc[128:256, :], cos, sin).astype(BF16)
    kv[4, 0:128, :] = rot(acc[256:384, :], cos, sin).astype(BF16)
    kv[4, 128:256, :] = acc[384:512, :].astype(BF16)

    def piece(slot, p):
        return kv.at[slot, p * 128 : (p + 1) * 128, :]

    def kv_out(slot, r, p):
        return pltpu.make_async_remote_copy(
            src_ref=piece(slot, p), dst_ref=piece(4 - r, p), send_sem=kv_s.at[p, r], recv_sem=kv_r.at[p, r],
            device_id=at_y(r), device_id_type=MESH,
        )

    def kv_up(p):
        return pltpu.make_async_remote_copy(
            src_ref=piece(4, p), dst_ref=piece(0, p), send_sem=kv_s.at[p, 0], recv_sem=kv_r.at[p, 0],
            device_id=at_z(1), device_id_type=MESH,
        )

    @pl.when(zh < 3)
    def _():
        kv_up(0).start()

    for p in (0, 1):
        for r in (1, 2, 3):

            @pl.when(y + r < 4)
            def _():
                kv_out(4, r, p).start()

    @pl.when(zh == 0)
    def _():
        kv[0] = jnp.zeros((256, T), BF16)

    @pl.when(zh < 3)
    def _():
        kv_up(0).wait_send()
        kv_up(1).start()

    def relay_kv(p):
        @pl.when(zh > 0)
        def _():
            kv_up(p).wait_recv()

        for r in (1, 2, 3):

            @pl.when(y + r >= 4)
            def _():
                kv_out(0, r, p).start()

    relay_kv(0)

    def kv_sent():
        for p in (0, 1):
            for r in (1, 2, 3):
                kv_out(0, r, p).wait_send()

        @pl.when(zh < 3)
        def _():
            kv_up(1).wait_send()

    tail.append(kv_sent)

    lane = lax.broadcasted_iota(jnp.int32, (1, T), 1)
    limit = jnp.minimum(jnp.minimum(pos_ref[...], WINDOW - 1), lane + c * T)
    limit = jnp.concatenate([limit, limit], axis=1)
    token = jnp.concatenate([lane, lane], axis=1)
    base = lax.broadcasted_iota(jnp.int32, (STEP, 2 * T), 0)
    gap = token - base
    neg = jnp.full((STEP, 2 * T), -jnp.inf, F32)

    highest = jnp.full((8, 2 * T), -jnp.inf, F32)
    for slot in (4, 0, 3, 1, 2):
        if slot == 3:
            relay_kv(1)
        if slot in (1, 2, 3):
            kv_out(0, 4 - slot, 0).wait_recv()
        s_scr[slot] = dot_tn(kv[slot, 0:128, :], qt[...])

        def mask(i, top, slot=slot):
            at = pl.multiple_of(i * STEP, STEP)
            distance = gap + ((4 - slot) * T - at)
            scores = s_scr[slot, pl.ds(at, STEP), :] * SCALE
            scores = jnp.where((distance >= 0) & (distance <= limit), scores, neg)
            s_scr[slot, pl.ds(at, STEP), :] = scores
            for j in range(0, STEP, 8):
                top = jnp.maximum(top, scores[j : j + 8])
            return top

        highest = lax.fori_loop(0, T // STEP, mask, highest)
    highest = jnp.max(highest, axis=0, keepdims=True)

    for r in (1, 2, 3):
        kv_out(0, r, 1).wait_recv()

    for r in (1, 2, 3):
        for j in range(2):
            dz = q * 2 + j
            send(
                xt.at[rows(dz * 4 + (y + r) % 4), :], xa.at[r - 1, dz], (xa_s, xa_r, 4), (r - 1) * 2 + j, at_y(r)
            )

    def expo(i, total):
        at = pl.multiple_of(i * STEP, STEP)
        slot, at = i // (T // STEP), pl.multiple_of((i % (T // STEP)) * STEP, STEP)
        e = jnp.exp(s_scr[slot, pl.ds(at, STEP), :] - highest)
        p_scr[slot, pl.ds(at, STEP), :] = e
        return total + fold(e)

    total = lax.fori_loop(0, 5 * T // STEP, expo, jnp.zeros((8, 2 * T), F32))
    recip = 1.0 / jnp.sum(total, axis=0, keepdims=True)

    def norm(i, carry):
        slot, at = i // (T // STEP), pl.multiple_of((i % (T // STEP)) * STEP, STEP)
        wt_scr[slot, pl.ds(at, STEP), :] = (p_scr[slot, pl.ds(at, STEP), :] * recip).astype(BF16)
        return carry

    lax.fori_loop(0, 5 * T // STEP, norm, 0)
    out = dot_nn(kv[0, 128:256, :], wt_scr[0])
    for slot in range(1, 5):
        out = out + dot_nn(kv[slot, 128:256, :], wt_scr[slot])
    out = out.astype(BF16)
    att[0:128, :] = out[:, 0:T]
    att[128:256, :] = out[:, T : 2 * T]
    att_all[c] = att[...]

    def project_out(chip):
        return dot_nn(wot[rows(chip, PAIR), :], att[...])

    out_first, out_second = scatter(project_out, 0)
    out_first()
    for r in (1, 2, 3):
        send(att, att_all.at[c], (at_s, at_r, 2), r, at_z(r))
    branch[...] = out_second()
    gain = gain_t[...]
    scaled = scaled_t[...]
    stat[h] = jnp.zeros((8, T), F32)
    stat[h, 0:1, :] = jnp.sum(branch[...] * branch[...], axis=0, keepdims=True)
    stat[h, 1:2, :] = jnp.sum(scaled * branch[...], axis=0, keepdims=True)
    for i, o in enumerate(others):
        send(stat.at[h], stat.at[h], (st_s, st_r, 3), i, at_head(o))

    for i, o in enumerate(others):
        back = head_of((o[0], (4 - o[1]) % 4, o[2]))
        landed(stat.at[back], (st_s, st_r, 3), i)
    sums = stat[0]
    for i in range(1, 16):
        sums = sums + stat[i]
    inverse = lax.rsqrt(sums[0:1] / D + EPSILON)
    slopes = inverse * sums[1:2] / D
    normed = branch[...] * inverse
    bg[rows(h), :] = (inverse * (scaled - normed * slopes)).astype(BF16)
    bg_begin, bg_finish, _, _ = gather(bg, (ag_s.at[1], ag_r.at[1], (0, 1)))
    bg_begin()
    for r in (1, 2, 3):
        source = ((zh + 4 - r) % 4) * 4 + y
        landed(att_all.at[source], (at_s, at_r, 2), r)
    for r in (1, 2, 3):
        for dz in range(4):
            block = att_all.at[((zh + dz) % 4) * 4 + y]
            i = 4 + (r - 1) * 4 + dz
            send(block, block, (at_s, at_r, 2), i, at_y(r))
    hidden_ref[...] = (x_ref[...].astype(F32) + normed * gain).astype(BF16)

    def mirror():
        return pltpu.make_async_remote_copy(
            src_ref=bg.at[rows(h), :], dst_ref=bgt.at[rows(c), :], send_sem=pm_s, recv_sem=pm_r,
            device_id=(h, c), device_id_type=MESH,
        )

    def mirrored():
        return pltpu.make_async_remote_copy(
            src_ref=bg.at[rows(h), :], dst_ref=bgt.at[rows(h), :], send_sem=pm_s, recv_sem=pm_r,
            device_id=(h, c), device_id_type=MESH,
        )

    @pl.when(c != h)
    def _():
        mirror().start()

    def mirror_sent():
        @pl.when(c != h)
        def _():
            mirror().wait_send()

    tail.append(mirror_sent)

    @pl.when(c == h)
    def _():
        bgt[rows(h), :] = bg[rows(h), :]

    acc[0:256, :] = jnp.zeros((256, T), F32)

    def project_back(chip):
        acc[0:256, :] += dot_tn(wot[rows(chip, PAIR), :], bg[rows(chip, PAIR), :])

    bg_finish(project_back)
    ga[:, 0:T] = acc[0:128, :].astype(BF16)
    ga[:, T : 2 * T] = acc[128:256, :].astype(BF16)

    for r in (1, 2, 3):
        for j in range(2):
            block = xa.at[r - 1, q * 2 + j]
            landed(block, (xa_s, xa_r, 4), (r - 1) * 2 + j)
            send(block, block, (xa_s, xa_r, 4), 6 + (r - 1) * 2 + j, at_head((0, 0, 1)))

    inner = jnp.zeros((8, 2 * T), F32)
    for slot in range(5):
        s_scr[slot] = dot_tn(kv[slot, 128:256, :], ga[...])

    def weigh(i, total):
        slot, at = i // (T // STEP), pl.multiple_of((i % (T // STEP)) * STEP, STEP)
        return total + fold(p_scr[slot, pl.ds(at, STEP), :] * s_scr[slot, pl.ds(at, STEP), :])

    inner = jnp.sum(lax.fori_loop(0, 5 * T // STEP, weigh, inner), axis=0, keepdims=True) * recip

    def grad(i, carry):
        slot, at = i // (T // STEP), pl.multiple_of((i % (T // STEP)) * STEP, STEP)
        p = p_scr[slot, pl.ds(at, STEP), :] * recip
        ds_scr[slot, pl.ds(at, STEP), :] = (p * (s_scr[slot, pl.ds(at, STEP), :] - inner)).astype(BF16)
        return carry

    lax.fori_loop(0, 5 * T // STEP, grad, 0)
    dq = dot_nn(kv[0, 0:128, :], ds_scr[0])
    for slot in range(1, 5):
        dq = dq + dot_nn(kv[slot, 0:128, :], ds_scr[slot])
    dq = dq * SCALE
    g_all[0, 0:128, :] = rot(dq[:, 0:T], cos, -sin).astype(BF16)
    g_all[0, 128:256, :] = rot(dq[:, T : 2 * T], cos, -sin).astype(BF16)
    for r in (1, 2, 3):
        send(
            g_all.at[0, 0:256, :], g_all.at[r, 0:256, :], (g_s, g_r, 6), r - 1, at_y(r)
        )

    for slot in (1, 2, 3, 0, 4):
        dk = dot_nt(qt[...], ds_scr[slot]) * SCALE
        dv = dot_nt(ga[...], wt_scr[slot])
        if slot in (1, 2, 3):
            halo_out[slot - 1, 0:128, :] = dk.astype(BF16)
            halo_out[slot - 1, 128:256, :] = dv.astype(BF16)
            send(
                halo_out.at[slot - 1], halo_in.at[slot - 1], (ha_s, ha_r, 5), slot, at_y(slot)
            )
        else:
            i = 0 if slot == 0 else 1
            halo_prev[i, 0:128, :] = dk
            halo_prev[i, 128:256, :] = dv
    @pl.when(c != h)
    def _():
        mirrored().wait_recv()

    bgt_begin, _, bgt_relays, bgt_takes = gather(bgt, (ag_s.at[2], ag_r.at[2], (0, 2)))
    bgt_begin()

    low, high = slice(0, HALF), slice(HALF, BLK)

    def weight_grads(k):
        sems = (dw_s.at[k], dw_r.at[k], (7, k))
        lo = k * 256
        up, far, back = dw_out.at[k * 3], dw_out.at[k * 3 + 1], dw_out.at[k * 3 + 2]
        mid, in_up, in_back = dw_in.at[k * 3], dw_in.at[k * 3 + 1], dw_in.at[k * 3 + 2]

        def product(dz):
            z = (zh + dz) % 4
            total = dot_nt(xt[rows(z * 4 + y), :], g_all[0, lo : lo + 256, :])
            for r in (1, 2, 3):
                total = total + dot_nt(xa[r - 1, z], g_all[r, lo : lo + 256, :])
            return total

        def begin():
            for r in (1, 2, 3):
                landed(g_all.at[r, lo : lo + 256, :], (g_s, g_r, 6), r - 1 + 3 * k)
            far[...] = product(2).astype(BF16)
            send(far.at[low, :], mid.at[low, :], sems, 0, at_z(1))
            send(far.at[high, :], mid.at[high, :], sems, 1, at_z(3))
            up[...] = product(1).astype(BF16)
            send(up.at[high, :], in_up.at[high, :], sems, 2, at_z(1))
            back[...] = product(3).astype(BF16)
            send(back.at[low, :], in_back.at[low, :], sems, 3, at_z(3))
            return product(0)

        def follow():
            landed(mid.at[low, :], sems, 0)
            up[low, :] = (up[low, :].astype(F32) + mid[low, :].astype(F32)).astype(BF16)
            send(up.at[low, :], in_up.at[low, :], sems, 4, at_z(1))
            landed(mid.at[high, :], sems, 1)
            back[high, :] = (back[high, :].astype(F32) + mid[high, :].astype(F32)).astype(BF16)
            send(back.at[high, :], in_back.at[high, :], sems, 5, at_z(3))

        def received():
            landed(in_up.at[high, :], sems, 2)
            landed(in_back.at[low, :], sems, 3)
            landed(in_up.at[low, :], sems, 4)
            landed(in_back.at[high, :], sems, 5)
            return in_up[...].astype(F32) + in_back[...].astype(F32)

        return begin, follow, received

    for r in (1, 2, 3):
        for j in range(2):
            landed(xa.at[r - 1, (1 - q) * 2 + j], (xa_s, xa_r, 4), 6 + (r - 1) * 2 + j)
    wq_begin, wq_follow, wq_received = weight_grads(0)
    wkv_begin, wkv_follow, wkv_received = weight_grads(1)
    dwq_ref[...] = wq_begin()

    for r in (1, 2, 3):
        landed(halo_in.at[r - 1], (ha_s, ha_r, 5), r)
        value = halo_in[r - 1].astype(F32)
        earlier = (y >= r).astype(F32)
        halo_prev[0] += value * earlier
        halo_prev[1] += value * (1.0 - earlier)
    halo_z[0] = halo_prev[0].astype(BF16)

    def down():
        return pltpu.make_async_remote_copy(
            src_ref=halo_z.at[0], dst_ref=halo_z.at[1], send_sem=ha_s.at[0], recv_sem=ha_r.at[0],
            device_id=at_z(3), device_id_type=MESH,
        )

    @pl.when(zh > 0)
    def _():
        down().start()

    def down_sent():
        @pl.when(zh > 0)
        def _():
            down().wait_send()

    tail.append(down_sent)
    bgt_relays(0, 4)
    wq_follow()

    @pl.when(zh < 3)
    def _():
        down().wait_recv()
        halo_prev[1] += halo_z[1].astype(F32)

    g_all[0, 256:384, :] = rot(halo_prev[1, 0:128, :], cos, -sin).astype(BF16)
    g_all[0, 384:512, :] = halo_prev[1, 128:256, :].astype(BF16)
    for r in (1, 2, 3):
        send(
            g_all.at[0, 256:512, :], g_all.at[r, 256:512, :], (g_s, g_r, 6), r + 2, at_y(r)
        )

    def input_terms(chip):
        return dot_nn(w[rows(chip, PAIR), :], g_all[0])

    in_first, in_second = scatter(input_terms, 1)
    in_first()
    dkv = wkv_begin()
    dwk_ref[...] = dkv[:, 0:128]
    dwv_ref[...] = dkv[:, 128:256]
    bgt_relays(4, 7)
    wkv_follow()
    gin_ref[...] = (cot_ref[...].astype(F32) + in_second()).astype(BF16)

    for r in (1, 2, 3):
        for dz in range(4):
            block = att_all.at[((zh + dz) % 4) * 4 + (y + 4 - r) % 4]
            i = 4 + (r - 1) * 4 + dz
            landed(block, (at_s, at_r, 2), i)
    dwo_ref[...] = jnp.zeros_like(dwo_ref)

    def out_grad(chip):
        for j in range(2):
            dwo_ref[...] += dot_nt(bgt[rows(chip * 2 + j), :], att_all[chip * 2 + j])

    bgt_takes(out_grad)

    dwq_ref[...] += wq_received()
    value = wkv_received()
    dwk_ref[...] += value[:, 0:128]
    dwv_ref[...] += value[:, 128:256]

    for copy in pending:
        copy.wait_send()
    for wait in tail:
        wait()


def settle(*refs):
    for i in range(6):
        refs[6 + i][...] = refs[i][...]


def local(inputs, positions, w_query, w_key, w_value, w_out, post_gain, cotangent):
    frequency = np.exp(np.arange(HD // 2, dtype=np.float32) * np.float32(-2.0 * math.log(ROPE_BASE) / HD))[:, None]
    vmem = pl.BlockSpec(memory_space=pltpu.VMEM)
    hbm = pl.BlockSpec(memory_space=pl.ANY)
    dma = pltpu.SemaphoreType.DMA
    scratch = [
        pltpu.VMEM((D, 512), BF16),
        pltpu.VMEM((256, D), BF16),
        pltpu.VMEM((D, 256), BF16),
        pltpu.VMEM((D, T), BF16),
        pltpu.VMEM((3, 4, BLK, T), BF16),
        pltpu.VMEM((2, D, T), BF16),
        pltpu.VMEM((D, T), BF16),
        pltpu.VMEM((D, T), BF16),
        pltpu.VMEM((16, 256, T), BF16),
        pltpu.VMEM((256, T), BF16),
        pltpu.VMEM((128, 2 * T), BF16),
        pltpu.VMEM((128, 2 * T), BF16),
        pltpu.VMEM((5, 256, T), BF16),
        pltpu.VMEM((5, T, 2 * T), F32),
        pltpu.VMEM((5, T, 2 * T), F32),
        pltpu.VMEM((5, T, 2 * T), BF16),
        pltpu.VMEM((4, 512, T), BF16),
        pltpu.VMEM((512, T), F32),
        pltpu.VMEM((2, 8, BLK, T), BF16),
        pltpu.VMEM((2, 4, BLK, T), BF16),
        pltpu.VMEM((2, BLK, T), BF16),
        pltpu.VMEM((2, 2, BLK, T), BF16),
        pltpu.VMEM((2, 8, BLK, T), BF16),
        pltpu.VMEM((BLK, T), F32),
        pltpu.VMEM((16, 8, T), F32),
        pltpu.VMEM((3, 256, T), BF16),
        pltpu.VMEM((3, 256, T), BF16),
        pltpu.VMEM((2, 256, T), F32),
        pltpu.VMEM((2, 256, T), BF16),
        pltpu.VMEM((6, BLK, T), BF16),
        pltpu.VMEM((6, BLK, T), BF16),
        pltpu.VMEM((2, HD // 2, T), F32),
        pltpu.VMEM((BLK, T), F32),
        pltpu.VMEM((BLK, T), F32),
        pltpu.VMEM((5, T, 2 * T), BF16),
        dma((4,)),
        dma((3, 16)), dma((3, 16)),
        dma((2, 15)), dma((2, 15)),
        dma((15,)), dma((15,)),
        dma((2, 4)), dma((2, 4)),
        dma((12,)), dma((12,)),
        dma((16,)), dma((16,)),
        dma, dma,
        dma((4,)), dma((4,)),
        dma((6,)), dma((6,)),
        dma((2, 6)), dma((2, 6)),
    ]
    shapes = (
        jax.ShapeDtypeStruct((BLK, T), BF16),
        jax.ShapeDtypeStruct((BLK, T), BF16),
        jax.ShapeDtypeStruct((BLK, 256), F32),
        jax.ShapeDtypeStruct((BLK, 128), F32),
        jax.ShapeDtypeStruct((BLK, 128), F32),
        jax.ShapeDtypeStruct((BLK, 256), F32),
    )
    results = pl.pallas_call(
        kernel,
        out_shape=shapes,
        in_specs=[vmem] * 5 + [hbm] * 4,
        out_specs=(vmem,) * 6,
        scratch_shapes=scratch,
        compiler_params=pltpu.CompilerParams(
            collective_id=0, has_side_effects=True, vmem_limit_bytes=60 * 1024 * 1024
        ),
        name="layer",
    )(
        inputs.T, cotangent.T, positions[None, :], post_gain, frequency,
        w_query, w_key, w_value, w_out,
    )
    hidden, gin, dwq, dwk, dwv, dwo = pl.pallas_call(
        settle,
        out_shape=shapes,
        in_specs=[vmem] * 6,
        out_specs=(vmem,) * 6,
        name="results",
    )(*results)
    return hidden.T, gin.T, dwq, dwk, dwv, dwo.T


def solution(mesh):
    in_specs = (
        P("ctx", "head"), P("ctx"), P(None, "head"), P(None, "head"),
        P(None, "head"), P("head", None), P("head"), P("ctx", "head"),
    )
    out_specs = (P("ctx", "head"),) * 5 + (P("head", "ctx"),)
    return jax.shard_map(local, mesh=mesh, in_specs=in_specs, out_specs=out_specs, check_vma=False)
```

```python
import functools
import math

import jax
import jax.numpy as jnp
import numpy as np
from jax import lax
from jax.experimental import pallas as pl
from jax.experimental.pallas import tpu as pltpu
from jax.sharding import PartitionSpec as P

D = 5376
HEADS = 32
WINDOW = 1024
EPSILON = 1e-06
ROPE_BASE = 10000.0
HD = 128
T = 256
BLK = 336
PAIR = 672
HALF = 176
MESH = pl.DeviceIdType.MESH
F32 = jnp.float32
BF16 = jnp.bfloat16
SCALE = (D // HEADS) ** (-0.5)
STEP = 32


def dot_nn(a, b):
    return lax.dot_general(a, b, (((1,), (0,)), ((), ())), preferred_element_type=F32)


def dot_nt(a, b):
    return lax.dot_general(a, b, (((1,), (1,)), ((), ())), preferred_element_type=F32)


def dot_tn(a, b):
    return lax.dot_general(a, b, (((0,), (0,)), ((), ())), preferred_element_type=F32)


def rot(v, cos, sin):
    half = HD // 2
    a, b = v[:half], v[half:]
    return jnp.concatenate([a * cos - b * sin, b * cos + a * sin], axis=0)


def fold(v):
    total = v[0:8]
    for i in range(8, v.shape[0], 8):
        total = total + v[i : i + 8]
    return total


def kernel(
    x_ref, cot_ref, pos_ref, gain_ref, freq_ref, wq_hbm, wk_hbm, wv_hbm, wo_hbm,
    hidden_ref, gin_ref, dwq_ref, dwk_ref, dwv_ref, dwo_ref,
    w, wo, wot, xt, xa, part, bg, bgt, att_all, att, qt, ga, kv, s_scr, p_scr, wt_scr, g_all,
    acc, r_core, r_x, r_x2, r_z, s_buf, branch, stat, halo_out, halo_in, halo_prev, halo_z, dw_out, dw_in,
    trig, gain_t, scaled_t,
    ds_scr,
    load_sem, ag_s, ag_r, rs_s, rs_r, st_s, st_r, kv_s, kv_r, xa_s, xa_r, at_s, at_r, pm_s, pm_r,
    ha_s, ha_r, g_s, g_r, dw_s, dw_r,
):
    c = lax.axis_index("ctx")
    h = lax.axis_index("head")
    zh, y = c // 4, c % 4
    zl, x, q = h // 8, (h // 2) % 4, h % 2

    def head_of(o):
        return ((zl + o[0]) % 2) * 8 + ((x + o[1]) % 4) * 2 + (q + o[2]) % 2

    def at_head(o):
        return (c, head_of(o))

    def at_y(r):
        return (zh * 4 + (y + r) % 4, h)

    def at_z(r):
        return (((zh + r) % 4) * 4 + y, h)

    def rows(index, size=BLK):
        return pl.ds(pl.multiple_of(index * size, 16), size)

    pending = []
    tail = []

    def send(src, dst, sems, k, device):
        copy = pltpu.make_async_remote_copy(
            src_ref=src, dst_ref=dst, send_sem=sems[0].at[k], recv_sem=sems[1].at[k],
            device_id=device, device_id_type=MESH,
        )
        copy.start()
        pending.append(copy)

    def landed(dst, sems, k):
        pltpu.make_async_remote_copy(
            src_ref=dst, dst_ref=dst, send_sem=sems[0].at[k], recv_sem=sems[1].at[k],
            device_id=at_y(1), device_id_type=MESH,
        ).wait_recv()


    loads = []
    for i, (src, dst) in enumerate(
        (
            (wq_hbm, w.at[:, 0:256]),
            (wk_hbm, w.at[:, 256:384]),
            (wv_hbm, w.at[:, 384:512]),
            (wo_hbm, wo),
        )
    ):
        cp = pltpu.make_async_copy(src, dst, load_sem.at[i])
        cp.start()
        loads.append(cp)
    xt[rows(h), :] = x_ref[...]

    barrier = pltpu.get_barrier_semaphore()
    others = [(a, b, d) for a in (0, 1) for b in range(4) for d in (0, 1) if (a, b, d) != (0, 0, 0)]
    for o in others:
        pl.semaphore_signal(barrier, inc=1, device_id=at_head(o), device_id_type=MESH)
    for r in (1, 2, 3):
        pl.semaphore_signal(barrier, inc=1, device_id=at_y(r), device_id_type=MESH)
        pl.semaphore_signal(barrier, inc=1, device_id=at_z(r), device_id_type=MESH)

    @pl.when(c != h)
    def _():
        pl.semaphore_signal(barrier, inc=1, device_id=(h, c), device_id_type=MESH)
        pl.semaphore_wait(barrier, 22)

    @pl.when(c == h)
    def _():
        pl.semaphore_wait(barrier, 21)

    def gather(buf, sems):
        def key(o):
            return o[0] * 8 + o[1] * 2 + o[2]

        def forward(o, e):
            rel = ((o[0] + e[0]) % 2, (o[1] - e[1]) % 4, (o[2] + e[2]) % 2)
            block = buf.at[rows(head_of(o)), :]
            send(block, block, sems, key(rel), at_head(e))

        def wait(o):
            block = buf.at[rows(head_of(o)), :]
            landed(block, sems, key(o))

        def begin():
            for e in ((1, 0, 0), (0, 1, 0), (0, 3, 0), (0, 2, 0), (0, 0, 1)):
                forward((0, 0, 0), e)

        events = (
            ((1, 0), ((0, 1, 0), (0, 3, 0), (0, 0, 1))),
            ((0, 1), ((0, 0, 1),)),
            ((0, 3), ((0, 0, 1),)),
            ((0, 2), ((1, 0, 0), (0, 0, 1))),
            ((1, 1), ((0, 0, 1),)),
            ((1, 3), ((0, 0, 1),)),
            ((1, 2), ((0, 0, 1),)),
        )

        def relay(chip, targets):
            wait((chip[0], chip[1], 0))
            for e in targets:
                forward((chip[0], chip[1], 0), e)

        def take(chip, consume):
            wait((chip[0], chip[1], 1))
            consume(head_of((chip[0], chip[1], 0)) // 2)

        def finish(consume):
            last = (0, 0)
            for chip, targets in events:
                relay(chip, targets)
                take(last, consume)
                last = chip
            take(last, consume)

        def relays(first, end):
            for chip, targets in events[first:end]:
                relay(chip, targets)

        def takes(consume):
            for chip in ((0, 0),) + tuple(chip for chip, _ in events):
                take(chip, consume)

        return begin, finish, relays, takes

    def scatter(produce, k):
        sems = (rs_s.at[k], rs_r.at[k], (1, k))
        rc, rx, rx2, rz, sb, pt = r_core.at[k], r_x.at[k], r_x2.at[k], r_z.at[k], s_buf.at[k], part.at[k]
        order = ((1, 2), (1, 1), (1, 3), (0, 1), (0, 3), (0, 2), (1, 0), (0, 0))

        def make(i):
            chip = head_of((order[i][0], order[i][1], 0)) // 2
            pt[rows(chip, PAIR), :] = produce(chip).astype(BF16)
            block = pt.at[rows(chip * 2 + 1 - q), :]
            send(block, rc.at[i], sems, i, at_head((0, 0, 1)))

        def settle(i):
            dz, dx = order[i]
            landed(rc.at[i], sems, i)
            total = pt[rows(head_of((dz, dx, 0))), :].astype(F32) + rc[i].astype(F32)
            if (dz, dx) == (1, 2):
                sb[i] = total.astype(BF16)
                send(sb.at[i], rz.at[0], sems, 8, at_head((1, 0, 0)))
            elif dx in (1, 3):
                j = (dx // 2) * 2 + dz
                sb[i] = total.astype(BF16)
                send(sb.at[i], rx.at[j], sems, 9 + j, at_head((0, dx, 0)))
            elif (dz, dx) == (0, 2):
                landed(rz.at[0], sems, 8)
                sb[i] = (total + rz[0].astype(F32)).astype(BF16)
                send(sb.at[i], rx2, sems, 13, at_head((0, 2, 0)))
            elif (dz, dx) == (1, 0):
                for j in (1, 3):
                    landed(rx.at[j], sems, 9 + j)
                    total = total + rx[j].astype(F32)
                sb[i] = total.astype(BF16)
                send(sb.at[i], rz.at[1], sems, 14, at_head((1, 0, 0)))
            else:
                for j in (0, 2):
                    landed(rx.at[j], sems, 9 + j)
                    total = total + rx[j].astype(F32)
                landed(rx2, sems, 13)
                total = total + rx2[...].astype(F32)
                landed(rz.at[1], sems, 14)
                total = total + rz[1].astype(F32)
                return total
            return None

        def first():
            for i in range(8):
                make(i)
                if 0 < i < 6:
                    settle(i - 1)

        def second():
            settle(5)
            settle(6)
            return settle(7)

        return first, second

    ag_begin, ag_finish, _, _ = gather(xt, (ag_s.at[0], ag_r.at[0], (0, 0)))
    ag_begin()
    acc[...] = jnp.zeros_like(acc)
    loads[3].wait()

    def turn(i, carry):
        at = pl.multiple_of(i * 128, 128)
        wot[pl.ds(at, 128), :] = wo[:, pl.ds(at, 128)].T
        return carry

    lax.fori_loop(0, D // 128, turn, 0)
    angles = freq_ref[...] * pos_ref[...].astype(F32)
    trig[0] = jnp.cos(angles)
    trig[1] = jnp.sin(angles)
    gain_t[...] = dot_tn(gain_ref[...].reshape(1, BLK), jnp.ones((1, T), BF16))
    scaled_t[...] = cot_ref[...].astype(F32) * gain_t[...]
    for cp in loads[:3]:
        cp.wait()

    def project(chip):
        acc[...] += dot_tn(w[rows(chip, PAIR), :], xt[rows(chip, PAIR), :])

    ag_finish(project)
    cos, sin = trig[0], trig[1]
    qt[:, 0:T] = rot(acc[0:128, :], cos, sin).astype(BF16)
    qt[:, T : 2 * T] = rot(acc[128:256, :], cos, sin).astype(BF16)
    kv[4, 0:128, :] = rot(acc[256:384, :], cos, sin).astype(BF16)
    kv[4, 128:256, :] = acc[384:512, :].astype(BF16)

    def piece(slot, p):
        return kv.at[slot, p * 128 : (p + 1) * 128, :]

    def kv_out(slot, r, p):
        return pltpu.make_async_remote_copy(
            src_ref=piece(slot, p), dst_ref=piece(4 - r, p), send_sem=kv_s.at[p, r], recv_sem=kv_r.at[p, r],
            device_id=at_y(r), device_id_type=MESH,
        )

    def kv_up(p):
        return pltpu.make_async_remote_copy(
            src_ref=piece(4, p), dst_ref=piece(0, p), send_sem=kv_s.at[p, 0], recv_sem=kv_r.at[p, 0],
            device_id=at_z(1), device_id_type=MESH,
        )

    @pl.when(zh < 3)
    def _():
        kv_up(0).start()

    for p in (0, 1):
        for r in (1, 2, 3):

            @pl.when(y + r < 4)
            def _():
                kv_out(4, r, p).start()

    @pl.when(zh == 0)
    def _():
        kv[0] = jnp.zeros((256, T), BF16)

    @pl.when(zh < 3)
    def _():
        kv_up(0).wait_send()
        kv_up(1).start()

    def relay_kv(p):
        @pl.when(zh > 0)
        def _():
            kv_up(p).wait_recv()

        for r in (1, 2, 3):

            @pl.when(y + r >= 4)
            def _():
                kv_out(0, r, p).start()

    relay_kv(0)

    def kv_sent():
        for p in (0, 1):
            for r in (1, 2, 3):
                kv_out(0, r, p).wait_send()

        @pl.when(zh < 3)
        def _():
            kv_up(1).wait_send()

    tail.append(kv_sent)

    lane = lax.broadcasted_iota(jnp.int32, (1, T), 1)
    limit = jnp.minimum(jnp.minimum(pos_ref[...], WINDOW - 1), lane + c * T)
    limit = jnp.concatenate([limit, limit], axis=1)
    token = jnp.concatenate([lane, lane], axis=1)
    base = lax.broadcasted_iota(jnp.int32, (STEP, 2 * T), 0)
    gap = token - base
    neg = jnp.full((STEP, 2 * T), -jnp.inf, F32)

    highest = jnp.full((8, 2 * T), -jnp.inf, F32)
    for slot in (4, 0, 3, 1, 2):
        if slot == 3:
            relay_kv(1)
        if slot in (1, 2, 3):
            kv_out(0, 4 - slot, 0).wait_recv()
        s_scr[slot] = dot_tn(kv[slot, 0:128, :], qt[...])

        def mask(i, top, slot=slot):
            at = pl.multiple_of(i * STEP, STEP)
            distance = gap + ((4 - slot) * T - at)
            scores = s_scr[slot, pl.ds(at, STEP), :] * SCALE
            scores = jnp.where((distance >= 0) & (distance <= limit), scores, neg)
            s_scr[slot, pl.ds(at, STEP), :] = scores
            for j in range(0, STEP, 8):
                top = jnp.maximum(top, scores[j : j + 8])
            return top

        highest = lax.fori_loop(0, T // STEP, mask, highest)
    highest = jnp.max(highest, axis=0, keepdims=True)

    for r in (1, 2, 3):
        kv_out(0, r, 1).wait_recv()

    for r in (1, 2, 3):
        for j in range(2):
            dz = q * 2 + j
            send(
                xt.at[rows(dz * 4 + (y + r) % 4), :], xa.at[r - 1, dz], (xa_s, xa_r, 4), (r - 1) * 2 + j, at_y(r)
            )

    def expo(i, total):
        at = pl.multiple_of(i * STEP, STEP)
        slot, at = i // (T // STEP), pl.multiple_of((i % (T // STEP)) * STEP, STEP)
        e = jnp.exp(s_scr[slot, pl.ds(at, STEP), :] - highest)
        p_scr[slot, pl.ds(at, STEP), :] = e
        return total + fold(e)

    total = lax.fori_loop(0, 5 * T // STEP, expo, jnp.zeros((8, 2 * T), F32))
    recip = 1.0 / jnp.sum(total, axis=0, keepdims=True)

    def norm(i, carry):
        slot, at = i // (T // STEP), pl.multiple_of((i % (T // STEP)) * STEP, STEP)
        wt_scr[slot, pl.ds(at, STEP), :] = (p_scr[slot, pl.ds(at, STEP), :] * recip).astype(BF16)
        return carry

    lax.fori_loop(0, 5 * T // STEP, norm, 0)
    out = dot_nn(kv[0, 128:256, :], wt_scr[0])
    for slot in range(1, 5):
        out = out + dot_nn(kv[slot, 128:256, :], wt_scr[slot])
    out = out.astype(BF16)
    att[0:128, :] = out[:, 0:T]
    att[128:256, :] = out[:, T : 2 * T]
    att_all[c] = att[...]

    def project_out(chip):
        return dot_nn(wot[rows(chip, PAIR), :], att[...])

    out_first, out_second = scatter(project_out, 0)
    out_first()
    for r in (1, 2, 3):
        send(att, att_all.at[c], (at_s, at_r, 2), r, at_z(r))

    def along_y(dz):
        block = att_all.at[((zh + dz) % 4) * 4 + y]
        for r in (1, 2, 3):
            send(block, block, (at_s, at_r, 2), 4 + (r - 1) * 4 + dz, at_y(r))

    along_y(0)
    branch[...] = out_second()
    gain = gain_t[...]
    scaled = scaled_t[...]
    stat[h] = jnp.zeros((8, T), F32)
    stat[h, 0:1, :] = jnp.sum(branch[...] * branch[...], axis=0, keepdims=True)
    stat[h, 1:2, :] = jnp.sum(scaled * branch[...], axis=0, keepdims=True)
    for i, o in enumerate(others):
        send(stat.at[h], stat.at[h], (st_s, st_r, 3), i, at_head(o))

    for i, o in enumerate(others):
        back = head_of((o[0], (4 - o[1]) % 4, o[2]))
        landed(stat.at[back], (st_s, st_r, 3), i)
    sums = stat[0]
    for i in range(1, 16):
        sums = sums + stat[i]
    inverse = lax.rsqrt(sums[0:1] / D + EPSILON)
    slopes = inverse * sums[1:2] / D
    normed = branch[...] * inverse
    bg[rows(h), :] = (inverse * (scaled - normed * slopes)).astype(BF16)
    bg_begin, bg_finish, _, _ = gather(bg, (ag_s.at[1], ag_r.at[1], (0, 1)))
    bg_begin()
    def attended_on(dz):
        landed(att_all.at[((zh + dz) % 4) * 4 + y], (at_s, at_r, 2), 4 - dz)
        along_y(dz)

    attended_on(3)
    attended_on(1)
    hidden_ref[...] = (x_ref[...].astype(F32) + normed * gain).astype(BF16)

    def mirror():
        return pltpu.make_async_remote_copy(
            src_ref=bg.at[rows(h), :], dst_ref=bgt.at[rows(c), :], send_sem=pm_s, recv_sem=pm_r,
            device_id=(h, c), device_id_type=MESH,
        )

    def mirrored():
        return pltpu.make_async_remote_copy(
            src_ref=bg.at[rows(h), :], dst_ref=bgt.at[rows(h), :], send_sem=pm_s, recv_sem=pm_r,
            device_id=(h, c), device_id_type=MESH,
        )

    @pl.when(c != h)
    def _():
        mirror().start()

    def mirror_sent():
        @pl.when(c != h)
        def _():
            mirror().wait_send()

    tail.append(mirror_sent)

    @pl.when(c == h)
    def _():
        bgt[rows(h), :] = bg[rows(h), :]

    acc[0:256, :] = jnp.zeros((256, T), F32)

    def project_back(chip):
        acc[0:256, :] += dot_tn(wot[rows(chip, PAIR), :], bg[rows(chip, PAIR), :])

    bg_finish(project_back)
    ga[:, 0:T] = acc[0:128, :].astype(BF16)
    ga[:, T : 2 * T] = acc[128:256, :].astype(BF16)

    for r in (1, 2, 3):
        for j in range(2):
            block = xa.at[r - 1, q * 2 + j]
            landed(block, (xa_s, xa_r, 4), (r - 1) * 2 + j)
            send(block, block, (xa_s, xa_r, 4), 6 + (r - 1) * 2 + j, at_head((0, 0, 1)))

    inner = jnp.zeros((8, 2 * T), F32)
    for slot in range(5):
        s_scr[slot] = dot_tn(kv[slot, 128:256, :], ga[...])

    def weigh(i, total):
        slot, at = i // (T // STEP), pl.multiple_of((i % (T // STEP)) * STEP, STEP)
        return total + fold(p_scr[slot, pl.ds(at, STEP), :] * s_scr[slot, pl.ds(at, STEP), :])

    inner = jnp.sum(lax.fori_loop(0, 5 * T // STEP, weigh, inner), axis=0, keepdims=True) * recip

    def grad(i, carry):
        slot, at = i // (T // STEP), pl.multiple_of((i % (T // STEP)) * STEP, STEP)
        p = p_scr[slot, pl.ds(at, STEP), :] * recip
        ds_scr[slot, pl.ds(at, STEP), :] = (p * (s_scr[slot, pl.ds(at, STEP), :] - inner)).astype(BF16)
        return carry

    lax.fori_loop(0, 5 * T // STEP, grad, 0)
    for slot in (1, 2, 3, 0, 4):
        dk = dot_nt(qt[...], ds_scr[slot]) * SCALE
        dv = dot_nt(ga[...], wt_scr[slot])
        if slot in (1, 2, 3):
            halo_out[slot - 1, 0:128, :] = dk.astype(BF16)
            halo_out[slot - 1, 128:256, :] = dv.astype(BF16)
            send(
                halo_out.at[slot - 1], halo_in.at[slot - 1], (ha_s, ha_r, 5), slot, at_y(slot)
            )
        else:
            i = 0 if slot == 0 else 1
            halo_prev[i, 0:128, :] = dk
            halo_prev[i, 128:256, :] = dv
    @pl.when(c != h)
    def _():
        mirrored().wait_recv()

    bgt_begin, _, bgt_relays, bgt_takes = gather(bgt, (ag_s.at[2], ag_r.at[2], (0, 2)))
    bgt_begin()

    dq = dot_nn(kv[0, 0:128, :], ds_scr[0])
    for slot in range(1, 5):
        dq = dq + dot_nn(kv[slot, 0:128, :], ds_scr[slot])
    dq = dq * SCALE
    g_all[0, 0:128, :] = rot(dq[:, 0:T], cos, -sin).astype(BF16)
    g_all[0, 128:256, :] = rot(dq[:, T : 2 * T], cos, -sin).astype(BF16)

    for r in (1, 2, 3):
        landed(halo_in.at[r - 1], (ha_s, ha_r, 5), r)
        value = halo_in[r - 1].astype(F32)
        earlier = (y >= r).astype(F32)
        halo_prev[0] += value * earlier
        halo_prev[1] += value * (1.0 - earlier)
    halo_z[0] = halo_prev[0].astype(BF16)

    def down():
        return pltpu.make_async_remote_copy(
            src_ref=halo_z.at[0], dst_ref=halo_z.at[1], send_sem=ha_s.at[0], recv_sem=ha_r.at[0],
            device_id=at_z(3), device_id_type=MESH,
        )

    @pl.when(zh > 0)
    def _():
        down().start()

    def down_sent():
        @pl.when(zh > 0)
        def _():
            down().wait_send()

    tail.append(down_sent)

    for r in (1, 2, 3):
        send(
            g_all.at[0, 0:256, :], g_all.at[r, 0:256, :], (g_s, g_r, 6), r - 1, at_y(r)
        )

    low, high = slice(0, HALF), slice(HALF, BLK)

    def weight_grads(k):
        sems = (dw_s.at[k], dw_r.at[k], (7, k))
        lo = k * 256
        up, far, back = dw_out.at[k * 3], dw_out.at[k * 3 + 1], dw_out.at[k * 3 + 2]
        mid, in_up, in_back = dw_in.at[k * 3], dw_in.at[k * 3 + 1], dw_in.at[k * 3 + 2]

        def product(dz):
            z = (zh + dz) % 4
            total = dot_nt(xt[rows(z * 4 + y), :], g_all[0, lo : lo + 256, :])
            for r in (1, 2, 3):
                total = total + dot_nt(xa[r - 1, z], g_all[r, lo : lo + 256, :])
            return total

        def begin():
            for r in (1, 2, 3):
                landed(g_all.at[r, lo : lo + 256, :], (g_s, g_r, 6), r - 1 + 3 * k)
            far[...] = product(2).astype(BF16)
            send(far.at[low, :], mid.at[low, :], sems, 0, at_z(1))
            send(far.at[high, :], mid.at[high, :], sems, 1, at_z(3))
            up[...] = product(1).astype(BF16)
            send(up.at[high, :], in_up.at[high, :], sems, 2, at_z(1))
            back[...] = product(3).astype(BF16)
            send(back.at[low, :], in_back.at[low, :], sems, 3, at_z(3))
            return product(0)

        def follow():
            landed(mid.at[low, :], sems, 0)
            up[low, :] = (up[low, :].astype(F32) + mid[low, :].astype(F32)).astype(BF16)
            send(up.at[low, :], in_up.at[low, :], sems, 4, at_z(1))
            landed(mid.at[high, :], sems, 1)
            back[high, :] = (back[high, :].astype(F32) + mid[high, :].astype(F32)).astype(BF16)
            send(back.at[high, :], in_back.at[high, :], sems, 5, at_z(3))

        def received():
            landed(in_up.at[high, :], sems, 2)
            landed(in_back.at[low, :], sems, 3)
            landed(in_up.at[low, :], sems, 4)
            landed(in_back.at[high, :], sems, 5)
            return in_up[...].astype(F32) + in_back[...].astype(F32)

        return begin, follow, received

    for r in (1, 2, 3):
        for j in range(2):
            landed(xa.at[r - 1, (1 - q) * 2 + j], (xa_s, xa_r, 4), 6 + (r - 1) * 2 + j)
    wq_begin, wq_follow, wq_received = weight_grads(0)
    wkv_begin, wkv_follow, wkv_received = weight_grads(1)
    bgt_relays(0, 4)

    @pl.when(zh < 3)
    def _():
        down().wait_recv()
        halo_prev[1] += halo_z[1].astype(F32)

    g_all[0, 256:384, :] = rot(halo_prev[1, 0:128, :], cos, -sin).astype(BF16)
    g_all[0, 384:512, :] = halo_prev[1, 128:256, :].astype(BF16)
    for r in (1, 2, 3):
        send(
            g_all.at[0, 256:512, :], g_all.at[r, 256:512, :], (g_s, g_r, 6), r + 2, at_y(r)
        )
    attended_on(2)

    dwq_ref[...] = wq_begin()

    def input_terms(chip):
        return dot_nn(w[rows(chip, PAIR), :], g_all[0])

    in_first, in_second = scatter(input_terms, 1)
    in_first()
    wq_follow()
    dkv = wkv_begin()
    dwk_ref[...] = dkv[:, 0:128]
    dwv_ref[...] = dkv[:, 128:256]
    bgt_relays(4, 7)
    wkv_follow()
    gin_ref[...] = (cot_ref[...].astype(F32) + in_second()).astype(BF16)

    for r in (1, 2, 3):
        for dz in range(4):
            block = att_all.at[((zh + dz) % 4) * 4 + (y + 4 - r) % 4]
            i = 4 + (r - 1) * 4 + dz
            landed(block, (at_s, at_r, 2), i)
    dwo_ref[...] = jnp.zeros_like(dwo_ref)

    def out_grad(chip):
        for j in range(2):
            dwo_ref[...] += dot_nt(bgt[rows(chip * 2 + j), :], att_all[chip * 2 + j])

    bgt_takes(out_grad)

    dwq_ref[...] += wq_received()
    value = wkv_received()
    dwk_ref[...] += value[:, 0:128]
    dwv_ref[...] += value[:, 128:256]

    for copy in pending:
        copy.wait_send()
    for wait in tail:
        wait()


def settle(*refs):
    for i in range(6):
        refs[6 + i][...] = refs[i][...]


def local(inputs, positions, w_query, w_key, w_value, w_out, post_gain, cotangent):
    frequency = np.exp(np.arange(HD // 2, dtype=np.float32) * np.float32(-2.0 * math.log(ROPE_BASE) / HD))[:, None]
    vmem = pl.BlockSpec(memory_space=pltpu.VMEM)
    hbm = pl.BlockSpec(memory_space=pl.ANY)
    dma = pltpu.SemaphoreType.DMA
    scratch = [
        pltpu.VMEM((D, 512), BF16),
        pltpu.VMEM((256, D), BF16),
        pltpu.VMEM((D, 256), BF16),
        pltpu.VMEM((D, T), BF16),
        pltpu.VMEM((3, 4, BLK, T), BF16),
        pltpu.VMEM((2, D, T), BF16),
        pltpu.VMEM((D, T), BF16),
        pltpu.VMEM((D, T), BF16),
        pltpu.VMEM((16, 256, T), BF16),
        pltpu.VMEM((256, T), BF16),
        pltpu.VMEM((128, 2 * T), BF16),
        pltpu.VMEM((128, 2 * T), BF16),
        pltpu.VMEM((5, 256, T), BF16),
        pltpu.VMEM((5, T, 2 * T), F32),
        pltpu.VMEM((5, T, 2 * T), F32),
        pltpu.VMEM((5, T, 2 * T), BF16),
        pltpu.VMEM((4, 512, T), BF16),
        pltpu.VMEM((512, T), F32),
        pltpu.VMEM((2, 8, BLK, T), BF16),
        pltpu.VMEM((2, 4, BLK, T), BF16),
        pltpu.VMEM((2, BLK, T), BF16),
        pltpu.VMEM((2, 2, BLK, T), BF16),
        pltpu.VMEM((2, 8, BLK, T), BF16),
        pltpu.VMEM((BLK, T), F32),
        pltpu.VMEM((16, 8, T), F32),
        pltpu.VMEM((3, 256, T), BF16),
        pltpu.VMEM((3, 256, T), BF16),
        pltpu.VMEM((2, 256, T), F32),
        pltpu.VMEM((2, 256, T), BF16),
        pltpu.VMEM((6, BLK, T), BF16),
        pltpu.VMEM((6, BLK, T), BF16),
        pltpu.VMEM((2, HD // 2, T), F32),
        pltpu.VMEM((BLK, T), F32),
        pltpu.VMEM((BLK, T), F32),
        pltpu.VMEM((5, T, 2 * T), BF16),
        dma((4,)),
        dma((3, 16)), dma((3, 16)),
        dma((2, 15)), dma((2, 15)),
        dma((15,)), dma((15,)),
        dma((2, 4)), dma((2, 4)),
        dma((12,)), dma((12,)),
        dma((16,)), dma((16,)),
        dma, dma,
        dma((4,)), dma((4,)),
        dma((6,)), dma((6,)),
        dma((2, 6)), dma((2, 6)),
    ]
    shapes = (
        jax.ShapeDtypeStruct((BLK, T), BF16),
        jax.ShapeDtypeStruct((BLK, T), BF16),
        jax.ShapeDtypeStruct((BLK, 256), F32),
        jax.ShapeDtypeStruct((BLK, 128), F32),
        jax.ShapeDtypeStruct((BLK, 128), F32),
        jax.ShapeDtypeStruct((BLK, 256), F32),
    )
    results = pl.pallas_call(
        kernel,
        out_shape=shapes,
        in_specs=[vmem] * 5 + [hbm] * 4,
        out_specs=(vmem,) * 6,
        scratch_shapes=scratch,
        compiler_params=pltpu.CompilerParams(
            collective_id=0, has_side_effects=True, vmem_limit_bytes=60 * 1024 * 1024
        ),
        name="layer",
    )(
        inputs.T, cotangent.T, positions[None, :], post_gain, frequency,
        w_query, w_key, w_value, w_out,
    )
    hidden, gin, dwq, dwk, dwv, dwo = pl.pallas_call(
        settle,
        out_shape=shapes,
        in_specs=[vmem] * 6,
        out_specs=(vmem,) * 6,
        name="results",
    )(*results)
    return hidden.T, gin.T, dwq, dwk, dwv, dwo.T


def solution(mesh):
    in_specs = (
        P("ctx", "head"), P("ctx"), P(None, "head"), P(None, "head"),
        P(None, "head"), P("head", None), P("head"), P("ctx", "head"),
    )
    out_specs = (P("ctx", "head"),) * 5 + (P("head", "ctx"),)
    return jax.shard_map(local, mesh=mesh, in_specs=in_specs, out_specs=out_specs, check_vma=False)
```

```python
import functools
import math

import jax
import jax.numpy as jnp
import numpy as np
from jax import lax
from jax.experimental import pallas as pl
from jax.experimental.pallas import tpu as pltpu
from jax.sharding import PartitionSpec as P

D = 5376
HEADS = 32
WINDOW = 1024
EPSILON = 1e-06
ROPE_BASE = 10000.0
HD = 128
T = 256
BLK = 336
PAIR = 672
HALF = 176
MESH = pl.DeviceIdType.MESH
F32 = jnp.float32
BF16 = jnp.bfloat16
SCALE = (D // HEADS) ** (-0.5)
STEP = 32


def dot_nn(a, b):
    return lax.dot_general(a, b, (((1,), (0,)), ((), ())), preferred_element_type=F32)


def dot_nt(a, b):
    return lax.dot_general(a, b, (((1,), (1,)), ((), ())), preferred_element_type=F32)


def dot_tn(a, b):
    return lax.dot_general(a, b, (((0,), (0,)), ((), ())), preferred_element_type=F32)


def rot(v, cos, sin):
    half = HD // 2
    a, b = v[:half], v[half:]
    return jnp.concatenate([a * cos - b * sin, b * cos + a * sin], axis=0)


def fold(v):
    total = v[0:8]
    for i in range(8, v.shape[0], 8):
        total = total + v[i : i + 8]
    return total


def kernel(
    x_ref, cot_ref, pos_ref, gain_ref, freq_ref, wq_hbm, wk_hbm, wv_hbm, wo_hbm,
    hidden_ref, gin_ref, dwq_ref, dwk_ref, dwv_ref, dwo_ref,
    w, wo, wot, xt, xa, part, bg, bgt, att_all, att, qt, ga, kv, s_scr, p_scr, wt_scr, g_all,
    acc, r_core, r_x, r_x2, r_z, s_buf, branch, stat, halo_out, halo_in, halo_prev, halo_z, dw_out, dw_in,
    trig, gain_t, scaled_t,
    ds_scr,
    load_sem, ag_s, ag_r, rs_s, rs_r, st_s, st_r, kv_s, kv_r, xa_s, xa_r, at_s, at_r, pm_s, pm_r,
    ha_s, ha_r, g_s, g_r, dw_s, dw_r,
):
    c = lax.axis_index("ctx")
    h = lax.axis_index("head")
    zh, y = c // 4, c % 4
    zl, x, q = h // 8, (h // 2) % 4, h % 2

    def head_of(o):
        return ((zl + o[0]) % 2) * 8 + ((x + o[1]) % 4) * 2 + (q + o[2]) % 2

    def at_head(o):
        return (c, head_of(o))

    def at_y(r):
        return (zh * 4 + (y + r) % 4, h)

    def at_z(r):
        return (((zh + r) % 4) * 4 + y, h)

    def rows(index, size=BLK):
        return pl.ds(pl.multiple_of(index * size, 16), size)

    pending = []
    tail = []

    def send(src, dst, sems, k, device):
        copy = pltpu.make_async_remote_copy(
            src_ref=src, dst_ref=dst, send_sem=sems[0].at[k], recv_sem=sems[1].at[k],
            device_id=device, device_id_type=MESH,
        )
        copy.start()
        pending.append(copy)

    def landed(dst, sems, k):
        pltpu.make_async_remote_copy(
            src_ref=dst, dst_ref=dst, send_sem=sems[0].at[k], recv_sem=sems[1].at[k],
            device_id=at_y(1), device_id_type=MESH,
        ).wait_recv()


    loads = []
    for i, (src, dst) in enumerate(
        (
            (wq_hbm, w.at[:, 0:256]),
            (wk_hbm, w.at[:, 256:384]),
            (wv_hbm, w.at[:, 384:512]),
            (wo_hbm, wo),
        )
    ):
        cp = pltpu.make_async_copy(src, dst, load_sem.at[i])
        cp.start()
        loads.append(cp)
    xt[rows(h), :] = x_ref[...]

    barrier = pltpu.get_barrier_semaphore()
    others = [(a, b, d) for a in (0, 1) for b in range(4) for d in (0, 1) if (a, b, d) != (0, 0, 0)]
    for o in others:
        pl.semaphore_signal(barrier, inc=1, device_id=at_head(o), device_id_type=MESH)
    for r in (1, 2, 3):
        pl.semaphore_signal(barrier, inc=1, device_id=at_y(r), device_id_type=MESH)
        pl.semaphore_signal(barrier, inc=1, device_id=at_z(r), device_id_type=MESH)

    @pl.when(c != h)
    def _():
        pl.semaphore_signal(barrier, inc=1, device_id=(h, c), device_id_type=MESH)
        pl.semaphore_wait(barrier, 22)

    @pl.when(c == h)
    def _():
        pl.semaphore_wait(barrier, 21)

    def gather(buf, sems):
        def key(o):
            return o[0] * 8 + o[1] * 2 + o[2]

        def forward(o, e):
            rel = ((o[0] + e[0]) % 2, (o[1] - e[1]) % 4, (o[2] + e[2]) % 2)
            block = buf.at[rows(head_of(o)), :]
            send(block, block, sems, key(rel), at_head(e))

        def wait(o):
            block = buf.at[rows(head_of(o)), :]
            landed(block, sems, key(o))

        def begin():
            for e in ((1, 0, 0), (0, 1, 0), (0, 3, 0), (0, 2, 0), (0, 0, 1)):
                forward((0, 0, 0), e)

        events = (
            ((1, 0), ((0, 1, 0), (0, 3, 0), (0, 0, 1))),
            ((0, 1), ((0, 0, 1),)),
            ((0, 3), ((0, 0, 1),)),
            ((0, 2), ((1, 0, 0), (0, 0, 1))),
            ((1, 1), ((0, 0, 1),)),
            ((1, 3), ((0, 0, 1),)),
            ((1, 2), ((0, 0, 1),)),
        )

        def relay(chip, targets):
            wait((chip[0], chip[1], 0))
            for e in targets:
                forward((chip[0], chip[1], 0), e)

        def take(chip, consume):
            wait((chip[0], chip[1], 1))
            consume(head_of((chip[0], chip[1], 0)) // 2)

        def finish(consume):
            chips = [chip for chip, _ in events]
            relays(0, 1)
            take((0, 0), consume)
            relays(1, 4)
            for i in range(7):
                if i in (2, 3, 4):
                    relays(i + 2, i + 3)
                take(chips[i], consume)

        def relays(first, end):
            for chip, targets in events[first:end]:
                relay(chip, targets)

        def takes(consume):
            for chip in ((0, 0),) + tuple(chip for chip, _ in events):
                take(chip, consume)

        return begin, finish, relays, takes

    def scatter(produce, k):
        sems = (rs_s.at[k], rs_r.at[k], (1, k))
        rc, rx, rx2, rz, sb, pt = r_core.at[k], r_x.at[k], r_x2.at[k], r_z.at[k], s_buf.at[k], part.at[k]
        order = ((1, 2), (1, 1), (1, 3), (0, 1), (0, 3), (0, 2), (1, 0), (0, 0))

        def make(i):
            chip = head_of((order[i][0], order[i][1], 0)) // 2
            pt[rows(chip, PAIR), :] = produce(chip).astype(BF16)
            block = pt.at[rows(chip * 2 + 1 - q), :]
            send(block, rc.at[i], sems, i, at_head((0, 0, 1)))

        def settle(i):
            dz, dx = order[i]
            landed(rc.at[i], sems, i)
            total = pt[rows(head_of((dz, dx, 0))), :].astype(F32) + rc[i].astype(F32)
            if (dz, dx) == (1, 2):
                sb[i] = total.astype(BF16)
                send(sb.at[i], rz.at[0], sems, 8, at_head((1, 0, 0)))
            elif dx in (1, 3):
                j = (dx // 2) * 2 + dz
                sb[i] = total.astype(BF16)
                send(sb.at[i], rx.at[j], sems, 9 + j, at_head((0, dx, 0)))
            elif (dz, dx) == (0, 2):
                landed(rz.at[0], sems, 8)
                sb[i] = (total + rz[0].astype(F32)).astype(BF16)
                send(sb.at[i], rx2, sems, 13, at_head((0, 2, 0)))
            elif (dz, dx) == (1, 0):
                for j in (1, 3):
                    landed(rx.at[j], sems, 9 + j)
                    total = total + rx[j].astype(F32)
                sb[i] = total.astype(BF16)
                send(sb.at[i], rz.at[1], sems, 14, at_head((1, 0, 0)))
            else:
                for j in (0, 2):
                    landed(rx.at[j], sems, 9 + j)
                    total = total + rx[j].astype(F32)
                landed(rx2, sems, 13)
                total = total + rx2[...].astype(F32)
                landed(rz.at[1], sems, 14)
                total = total + rz[1].astype(F32)
                return total
            return None

        def first():
            for i in range(8):
                make(i)
                if 0 < i < 6:
                    settle(i - 1)

        def second():
            settle(5)
            settle(6)
            return settle(7)

        return first, second

    ag_begin, ag_finish, _, _ = gather(xt, (ag_s.at[0], ag_r.at[0], (0, 0)))
    ag_begin()
    acc[...] = jnp.zeros_like(acc)
    loads[3].wait()

    def turn(i, carry):
        at = pl.multiple_of(i * 128, 128)
        wot[pl.ds(at, 128), :] = wo[:, pl.ds(at, 128)].T
        return carry

    lax.fori_loop(0, D // 128, turn, 0)
    angles = freq_ref[...] * pos_ref[...].astype(F32)
    trig[0] = jnp.cos(angles)
    trig[1] = jnp.sin(angles)
    gain_t[...] = dot_tn(gain_ref[...].reshape(1, BLK), jnp.ones((1, T), BF16))
    scaled_t[...] = cot_ref[...].astype(F32) * gain_t[...]
    for cp in loads[:3]:
        cp.wait()

    def project(chip):
        acc[...] += dot_tn(w[rows(chip, PAIR), :], xt[rows(chip, PAIR), :])

    ag_finish(project)
    cos, sin = trig[0], trig[1]
    qt[:, 0:T] = rot(acc[0:128, :], cos, sin).astype(BF16)
    qt[:, T : 2 * T] = rot(acc[128:256, :], cos, sin).astype(BF16)
    kv[4, 0:128, :] = rot(acc[256:384, :], cos, sin).astype(BF16)
    kv[4, 128:256, :] = acc[384:512, :].astype(BF16)

    def piece(slot, p):
        return kv.at[slot, p * 128 : (p + 1) * 128, :]

    def kv_out(slot, r, p):
        return pltpu.make_async_remote_copy(
            src_ref=piece(slot, p), dst_ref=piece(4 - r, p), send_sem=kv_s.at[p, r], recv_sem=kv_r.at[p, r],
            device_id=at_y(r), device_id_type=MESH,
        )

    def kv_up(p):
        return pltpu.make_async_remote_copy(
            src_ref=piece(4, p), dst_ref=piece(0, p), send_sem=kv_s.at[p, 0], recv_sem=kv_r.at[p, 0],
            device_id=at_z(1), device_id_type=MESH,
        )

    @pl.when(zh < 3)
    def _():
        kv_up(0).start()

    for p in (0, 1):
        for r in (1, 2, 3):

            @pl.when(y + r < 4)
            def _():
                kv_out(4, r, p).start()

    @pl.when(zh == 0)
    def _():
        kv[0] = jnp.zeros((256, T), BF16)

    @pl.when(zh < 3)
    def _():
        kv_up(0).wait_send()
        kv_up(1).start()

    def relay_kv(p):
        @pl.when(zh > 0)
        def _():
            kv_up(p).wait_recv()

        for r in (1, 2, 3):

            @pl.when(y + r >= 4)
            def _():
                kv_out(0, r, p).start()

    relay_kv(0)

    def kv_sent():
        for p in (0, 1):
            for r in (1, 2, 3):
                kv_out(0, r, p).wait_send()

        @pl.when(zh < 3)
        def _():
            kv_up(1).wait_send()

    tail.append(kv_sent)

    lane = lax.broadcasted_iota(jnp.int32, (1, T), 1)
    limit = jnp.minimum(jnp.minimum(pos_ref[...], WINDOW - 1), lane + c * T)
    limit = jnp.concatenate([limit, limit], axis=1)
    token = jnp.concatenate([lane, lane], axis=1)
    base = lax.broadcasted_iota(jnp.int32, (STEP, 2 * T), 0)
    gap = token - base
    neg = jnp.full((STEP, 2 * T), -jnp.inf, F32)

    highest = jnp.full((8, 2 * T), -jnp.inf, F32)
    for slot in (4, 0, 3, 1, 2):
        if slot == 3:
            relay_kv(1)
        if slot in (1, 2, 3):
            kv_out(0, 4 - slot, 0).wait_recv()
        s_scr[slot] = dot_tn(kv[slot, 0:128, :], qt[...])

        def mask(i, top, slot=slot):
            at = pl.multiple_of(i * STEP, STEP)
            distance = gap + ((4 - slot) * T - at)
            scores = s_scr[slot, pl.ds(at, STEP), :] * SCALE
            scores = jnp.where((distance >= 0) & (distance <= limit), scores, neg)
            s_scr[slot, pl.ds(at, STEP), :] = scores
            for j in range(0, STEP, 8):
                top = jnp.maximum(top, scores[j : j + 8])
            return top

        highest = lax.fori_loop(0, T // STEP, mask, highest)
    highest = jnp.max(highest, axis=0, keepdims=True)

    for r in (1, 2, 3):
        kv_out(0, r, 1).wait_recv()

    for r in (1, 2, 3):
        for j in range(2):
            dz = q * 2 + j
            send(
                xt.at[rows(dz * 4 + (y + r) % 4), :], xa.at[r - 1, dz], (xa_s, xa_r, 4), (r - 1) * 2 + j, at_y(r)
            )

    def expo(i, total):
        at = pl.multiple_of(i * STEP, STEP)
        slot, at = i // (T // STEP), pl.multiple_of((i % (T // STEP)) * STEP, STEP)
        e = jnp.exp(s_scr[slot, pl.ds(at, STEP), :] - highest)
        p_scr[slot, pl.ds(at, STEP), :] = e
        return total + fold(e)

    total = lax.fori_loop(0, 5 * T // STEP, expo, jnp.zeros((8, 2 * T), F32))
    recip = 1.0 / jnp.sum(total, axis=0, keepdims=True)

    def norm(i, carry):
        slot, at = i // (T // STEP), pl.multiple_of((i % (T // STEP)) * STEP, STEP)
        wt_scr[slot, pl.ds(at, STEP), :] = (p_scr[slot, pl.ds(at, STEP), :] * recip).astype(BF16)
        return carry

    lax.fori_loop(0, 5 * T // STEP, norm, 0)
    out = dot_nn(kv[0, 128:256, :], wt_scr[0])
    for slot in range(1, 5):
        out = out + dot_nn(kv[slot, 128:256, :], wt_scr[slot])
    out = out.astype(BF16)
    att[0:128, :] = out[:, 0:T]
    att[128:256, :] = out[:, T : 2 * T]
    att_all[c] = att[...]

    def project_out(chip):
        return dot_nn(wot[rows(chip, PAIR), :], att[...])

    out_first, out_second = scatter(project_out, 0)
    out_first()
    for r in (1, 2, 3):
        send(att, att_all.at[c], (at_s, at_r, 2), r, at_z(r))

    def along_y(dz):
        block = att_all.at[((zh + dz) % 4) * 4 + y]
        for r in (1, 2, 3):
            send(block, block, (at_s, at_r, 2), 4 + (r - 1) * 4 + dz, at_y(r))

    along_y(0)
    branch[...] = out_second()
    gain = gain_t[...]
    scaled = scaled_t[...]
    stat[h] = jnp.zeros((8, T), F32)
    stat[h, 0:1, :] = jnp.sum(branch[...] * branch[...], axis=0, keepdims=True)
    stat[h, 1:2, :] = jnp.sum(scaled * branch[...], axis=0, keepdims=True)
    for i, o in enumerate(others):
        send(stat.at[h], stat.at[h], (st_s, st_r, 3), i, at_head(o))

    for i, o in enumerate(others):
        back = head_of((o[0], (4 - o[1]) % 4, o[2]))
        landed(stat.at[back], (st_s, st_r, 3), i)
    sums = stat[0]
    for i in range(1, 16):
        sums = sums + stat[i]
    inverse = lax.rsqrt(sums[0:1] / D + EPSILON)
    slopes = inverse * sums[1:2] / D
    normed = branch[...] * inverse
    bg[rows(h), :] = (inverse * (scaled - normed * slopes)).astype(BF16)
    bg_begin, bg_finish, _, _ = gather(bg, (ag_s.at[1], ag_r.at[1], (0, 1)))
    bg_begin()
    def attended_on(dz):
        landed(att_all.at[((zh + dz) % 4) * 4 + y], (at_s, at_r, 2), 4 - dz)
        along_y(dz)

    attended_on(3)
    attended_on(1)
    hidden_ref[...] = (x_ref[...].astype(F32) + normed * gain).astype(BF16)

    def mirror():
        return pltpu.make_async_remote_copy(
            src_ref=bg.at[rows(h), :], dst_ref=bgt.at[rows(c), :], send_sem=pm_s, recv_sem=pm_r,
            device_id=(h, c), device_id_type=MESH,
        )

    def mirrored():
        return pltpu.make_async_remote_copy(
            src_ref=bg.at[rows(h), :], dst_ref=bgt.at[rows(h), :], send_sem=pm_s, recv_sem=pm_r,
            device_id=(h, c), device_id_type=MESH,
        )

    @pl.when(c != h)
    def _():
        mirror().start()

    def mirror_sent():
        @pl.when(c != h)
        def _():
            mirror().wait_send()

    tail.append(mirror_sent)

    @pl.when(c == h)
    def _():
        bgt[rows(h), :] = bg[rows(h), :]

    acc[0:256, :] = jnp.zeros((256, T), F32)

    def project_back(chip):
        acc[0:256, :] += dot_tn(wot[rows(chip, PAIR), :], bg[rows(chip, PAIR), :])

    bg_finish(project_back)
    ga[:, 0:T] = acc[0:128, :].astype(BF16)
    ga[:, T : 2 * T] = acc[128:256, :].astype(BF16)

    for r in (1, 2, 3):
        for j in range(2):
            block = xa.at[r - 1, q * 2 + j]
            landed(block, (xa_s, xa_r, 4), (r - 1) * 2 + j)
            send(block, block, (xa_s, xa_r, 4), 6 + (r - 1) * 2 + j, at_head((0, 0, 1)))

    inner = jnp.zeros((8, 2 * T), F32)
    for slot in range(5):
        s_scr[slot] = dot_tn(kv[slot, 128:256, :], ga[...])

    def weigh(i, total):
        slot, at = i // (T // STEP), pl.multiple_of((i % (T // STEP)) * STEP, STEP)
        return total + fold(p_scr[slot, pl.ds(at, STEP), :] * s_scr[slot, pl.ds(at, STEP), :])

    inner = jnp.sum(lax.fori_loop(0, 5 * T // STEP, weigh, inner), axis=0, keepdims=True) * recip

    def grad(i, carry):
        slot, at = i // (T // STEP), pl.multiple_of((i % (T // STEP)) * STEP, STEP)
        p = p_scr[slot, pl.ds(at, STEP), :] * recip
        ds_scr[slot, pl.ds(at, STEP), :] = (p * (s_scr[slot, pl.ds(at, STEP), :] - inner)).astype(BF16)
        return carry

    lax.fori_loop(0, 5 * T // STEP, grad, 0)
    for slot in (1, 2, 3, 0, 4):
        dk = dot_nt(qt[...], ds_scr[slot]) * SCALE
        dv = dot_nt(ga[...], wt_scr[slot])
        if slot in (1, 2, 3):
            halo_out[slot - 1, 0:128, :] = dk.astype(BF16)
            halo_out[slot - 1, 128:256, :] = dv.astype(BF16)
            send(
                halo_out.at[slot - 1], halo_in.at[slot - 1], (ha_s, ha_r, 5), slot, at_y(slot)
            )
        else:
            i = 0 if slot == 0 else 1
            halo_prev[i, 0:128, :] = dk
            halo_prev[i, 128:256, :] = dv
    @pl.when(c != h)
    def _():
        mirrored().wait_recv()

    bgt_begin, _, bgt_relays, bgt_takes = gather(bgt, (ag_s.at[2], ag_r.at[2], (0, 2)))
    bgt_begin()

    dq = dot_nn(kv[0, 0:128, :], ds_scr[0])
    for slot in range(1, 5):
        dq = dq + dot_nn(kv[slot, 0:128, :], ds_scr[slot])
    dq = dq * SCALE
    g_all[0, 0:128, :] = rot(dq[:, 0:T], cos, -sin).astype(BF16)
    g_all[0, 128:256, :] = rot(dq[:, T : 2 * T], cos, -sin).astype(BF16)

    for r in (1, 2, 3):
        landed(halo_in.at[r - 1], (ha_s, ha_r, 5), r)
        value = halo_in[r - 1].astype(F32)
        earlier = (y >= r).astype(F32)
        halo_prev[0] += value * earlier
        halo_prev[1] += value * (1.0 - earlier)
    halo_z[0] = halo_prev[0].astype(BF16)

    def down():
        return pltpu.make_async_remote_copy(
            src_ref=halo_z.at[0], dst_ref=halo_z.at[1], send_sem=ha_s.at[0], recv_sem=ha_r.at[0],
            device_id=at_z(3), device_id_type=MESH,
        )

    @pl.when(zh > 0)
    def _():
        down().start()

    def down_sent():
        @pl.when(zh > 0)
        def _():
            down().wait_send()

    tail.append(down_sent)

    for r in (1, 2, 3):
        send(
            g_all.at[0, 0:256, :], g_all.at[r, 0:256, :], (g_s, g_r, 6), r - 1, at_y(r)
        )

    low, high = slice(0, HALF), slice(HALF, BLK)

    def weight_grads(k):
        sems = (dw_s.at[k], dw_r.at[k], (7, k))
        lo = k * 256
        up, far, back = dw_out.at[k * 3], dw_out.at[k * 3 + 1], dw_out.at[k * 3 + 2]
        mid, in_up, in_back = dw_in.at[k * 3], dw_in.at[k * 3 + 1], dw_in.at[k * 3 + 2]

        def product(dz):
            z = (zh + dz) % 4
            total = dot_nt(xt[rows(z * 4 + y), :], g_all[0, lo : lo + 256, :])
            for r in (1, 2, 3):
                total = total + dot_nt(xa[r - 1, z], g_all[r, lo : lo + 256, :])
            return total

        def begin():
            for r in (1, 2, 3):
                landed(g_all.at[r, lo : lo + 256, :], (g_s, g_r, 6), r - 1 + 3 * k)
            far[...] = product(2).astype(BF16)
            send(far.at[low, :], mid.at[low, :], sems, 0, at_z(1))
            send(far.at[high, :], mid.at[high, :], sems, 1, at_z(3))
            up[...] = product(1).astype(BF16)
            send(up.at[high, :], in_up.at[high, :], sems, 2, at_z(1))
            back[...] = product(3).astype(BF16)
            send(back.at[low, :], in_back.at[low, :], sems, 3, at_z(3))
            return product(0)

        def follow():
            landed(mid.at[low, :], sems, 0)
            up[low, :] = (up[low, :].astype(F32) + mid[low, :].astype(F32)).astype(BF16)
            send(up.at[low, :], in_up.at[low, :], sems, 4, at_z(1))
            landed(mid.at[high, :], sems, 1)
            back[high, :] = (back[high, :].astype(F32) + mid[high, :].astype(F32)).astype(BF16)
            send(back.at[high, :], in_back.at[high, :], sems, 5, at_z(3))

        def received():
            landed(in_up.at[high, :], sems, 2)
            landed(in_back.at[low, :], sems, 3)
            landed(in_up.at[low, :], sems, 4)
            landed(in_back.at[high, :], sems, 5)
            return in_up[...].astype(F32) + in_back[...].astype(F32)

        return begin, follow, received

    for r in (1, 2, 3):
        for j in range(2):
            landed(xa.at[r - 1, (1 - q) * 2 + j], (xa_s, xa_r, 4), 6 + (r - 1) * 2 + j)
    wq_begin, wq_follow, wq_received = weight_grads(0)
    wkv_begin, wkv_follow, wkv_received = weight_grads(1)
    bgt_relays(0, 4)

    @pl.when(zh < 3)
    def _():
        down().wait_recv()
        halo_prev[1] += halo_z[1].astype(F32)

    g_all[0, 256:384, :] = rot(halo_prev[1, 0:128, :], cos, -sin).astype(BF16)
    g_all[0, 384:512, :] = halo_prev[1, 128:256, :].astype(BF16)
    for r in (1, 2, 3):
        send(
            g_all.at[0, 256:512, :], g_all.at[r, 256:512, :], (g_s, g_r, 6), r + 2, at_y(r)
        )
    attended_on(2)

    dwq_ref[...] = wq_begin()

    def input_terms(chip):
        return dot_nn(w[rows(chip, PAIR), :], g_all[0])

    in_first, in_second = scatter(input_terms, 1)
    in_first()
    dkv = wkv_begin()
    dwk_ref[...] = dkv[:, 0:128]
    dwv_ref[...] = dkv[:, 128:256]
    wq_follow()
    bgt_relays(4, 7)
    wkv_follow()
    gin_ref[...] = (cot_ref[...].astype(F32) + in_second()).astype(BF16)

    for r in (1, 2, 3):
        for dz in range(4):
            block = att_all.at[((zh + dz) % 4) * 4 + (y + 4 - r) % 4]
            i = 4 + (r - 1) * 4 + dz
            landed(block, (at_s, at_r, 2), i)
    dwo_ref[...] = jnp.zeros_like(dwo_ref)

    def out_grad(chip):
        for j in range(2):
            dwo_ref[...] += dot_nt(bgt[rows(chip * 2 + j), :], att_all[chip * 2 + j])

    bgt_takes(out_grad)

    dwq_ref[...] += wq_received()
    value = wkv_received()
    dwk_ref[...] += value[:, 0:128]
    dwv_ref[...] += value[:, 128:256]

    for copy in pending:
        copy.wait_send()
    for wait in tail:
        wait()


def settle(*refs):
    sources, results, held = refs[0:6], refs[6:12], refs[12:18]
    in_sem, out_sem = refs[18], refs[19]
    ins = [pltpu.make_async_copy(sources[i], held[i], in_sem.at[i]) for i in range(6)]
    outs = [pltpu.make_async_copy(held[i], results[i], out_sem.at[i]) for i in range(6)]
    for copy in ins:
        copy.start()
    for i in range(6):
        ins[i].wait()
        outs[i].start()
    for copy in outs:
        copy.wait()


def local(inputs, positions, w_query, w_key, w_value, w_out, post_gain, cotangent):
    frequency = np.exp(np.arange(HD // 2, dtype=np.float32) * np.float32(-2.0 * math.log(ROPE_BASE) / HD))[:, None]
    vmem = pl.BlockSpec(memory_space=pltpu.VMEM)
    hbm = pl.BlockSpec(memory_space=pl.ANY)
    dma = pltpu.SemaphoreType.DMA
    scratch = [
        pltpu.VMEM((D, 512), BF16),
        pltpu.VMEM((256, D), BF16),
        pltpu.VMEM((D, 256), BF16),
        pltpu.VMEM((D, T), BF16),
        pltpu.VMEM((3, 4, BLK, T), BF16),
        pltpu.VMEM((2, D, T), BF16),
        pltpu.VMEM((D, T), BF16),
        pltpu.VMEM((D, T), BF16),
        pltpu.VMEM((16, 256, T), BF16),
        pltpu.VMEM((256, T), BF16),
        pltpu.VMEM((128, 2 * T), BF16),
        pltpu.VMEM((128, 2 * T), BF16),
        pltpu.VMEM((5, 256, T), BF16),
        pltpu.VMEM((5, T, 2 * T), F32),
        pltpu.VMEM((5, T, 2 * T), F32),
        pltpu.VMEM((5, T, 2 * T), BF16),
        pltpu.VMEM((4, 512, T), BF16),
        pltpu.VMEM((512, T), F32),
        pltpu.VMEM((2, 8, BLK, T), BF16),
        pltpu.VMEM((2, 4, BLK, T), BF16),
        pltpu.VMEM((2, BLK, T), BF16),
        pltpu.VMEM((2, 2, BLK, T), BF16),
        pltpu.VMEM((2, 8, BLK, T), BF16),
        pltpu.VMEM((BLK, T), F32),
        pltpu.VMEM((16, 8, T), F32),
        pltpu.VMEM((3, 256, T), BF16),
        pltpu.VMEM((3, 256, T), BF16),
        pltpu.VMEM((2, 256, T), F32),
        pltpu.VMEM((2, 256, T), BF16),
        pltpu.VMEM((6, BLK, T), BF16),
        pltpu.VMEM((6, BLK, T), BF16),
        pltpu.VMEM((2, HD // 2, T), F32),
        pltpu.VMEM((BLK, T), F32),
        pltpu.VMEM((BLK, T), F32),
        pltpu.VMEM((5, T, 2 * T), BF16),
        dma((4,)),
        dma((3, 16)), dma((3, 16)),
        dma((2, 15)), dma((2, 15)),
        dma((15,)), dma((15,)),
        dma((2, 4)), dma((2, 4)),
        dma((12,)), dma((12,)),
        dma((16,)), dma((16,)),
        dma, dma,
        dma((4,)), dma((4,)),
        dma((6,)), dma((6,)),
        dma((2, 6)), dma((2, 6)),
    ]
    shapes = (
        jax.ShapeDtypeStruct((BLK, T), BF16),
        jax.ShapeDtypeStruct((BLK, T), BF16),
        jax.ShapeDtypeStruct((BLK, 256), F32),
        jax.ShapeDtypeStruct((BLK, 128), F32),
        jax.ShapeDtypeStruct((BLK, 128), F32),
        jax.ShapeDtypeStruct((BLK, 256), F32),
    )
    results = pl.pallas_call(
        kernel,
        out_shape=shapes,
        in_specs=[vmem] * 5 + [hbm] * 4,
        out_specs=(vmem,) * 6,
        scratch_shapes=scratch,
        compiler_params=pltpu.CompilerParams(
            collective_id=0, has_side_effects=True, vmem_limit_bytes=60 * 1024 * 1024
        ),
        name="layer",
    )(
        inputs.T, cotangent.T, positions[None, :], post_gain, frequency,
        w_query, w_key, w_value, w_out,
    )
    hidden, gin, dwq, dwk, dwv, dwo = pl.pallas_call(
        settle,
        out_shape=shapes,
        in_specs=[hbm] * 6,
        out_specs=(hbm,) * 6,
        scratch_shapes=[pltpu.VMEM(shape.shape, shape.dtype) for shape in shapes] + [dma((6,)), dma((6,))],
        name="results",
    )(*results)
    return hidden.T, gin.T, dwq, dwk, dwv, dwo.T


def solution(mesh):
    in_specs = (
        P("ctx", "head"), P("ctx"), P(None, "head"), P(None, "head"),
        P(None, "head"), P("head", None), P("head"), P("ctx", "head"),
    )
    out_specs = (P("ctx", "head"),) * 5 + (P("head", "ctx"),)
    return jax.shard_map(local, mesh=mesh, in_specs=in_specs, out_specs=out_specs, check_vma=False)
```
